128 devices in a mesh: trans: 16 (over z_lo, x, core), pw: 8 (over z_hi, y).
Axes of the slice: x: 4, y: 4, z: 4 (z_hi: 2, z_lo: 2; z = z_hi * 2 + z_lo), core: 2. Of those that a mesh axis runs over, the one named last changes fastest.
Arguments:
- densities: bfloat16 [65536, 5120], P('trans', 'pw'), may hold values from -1.75 to 1.75
- coulomb: float32 [5120], P('pw'), may hold values from 0.25 to 4
- pairs: int32 [288, 2], replicated, may hold values from 0 to 127, as said below
- owner: int32 [128], replicated, may hold values from 0 to 127, as said below
Outputs:
- kernel: float32 [512, 288, 512], P('pw', 'trans')
- kernel_t: float32 [512, 288, 512], P('pw', 'trans')
The draws below stay inside these ranges and needn't reach their ends.
Inputs may be any that keep to these rules, and one draw needn't show every extreme that they name: `pairs`: pair p lists its first block at owner p // 18. Write s_q for (owner of the second block minus owner of the first) taken modulo 16 into -2 to 2; it depends only on the list position q = p % 18, the same for every owner. The value 0 is taken by 6 positions, each other value by exactly 3 positions. `owner`: A permutation of the 128 storage slots.
All inputs are finite; a program needn't handle non-finite values.
Results may differ from the reference program's by a relative error of at most 0.0027.
Values may be sent and summed in bfloat16 or wider, within the bound.
No kernel may reach another device: no remote copies, remote signals or barrier semaphores. Data moves between devices by JAX's collectives and lax.ppermute only.
A program may use at most 192 MiB of HBM per device.

```python
import math
import jax
import jax.numpy as jnp
from jax import lax

G = 5120
BLK = 512
BLK_DEV = 8
SPAN = 2
MULT = 3
PAIR_DEV = 18
NB = 128
PAIRS = 288
NT = 65536
N_PW = 8


def common_layout(key):
    keys = jax.random.split(key, 4)
    ntrans = NB // BLK_DEV
    owner = jax.random.permutation(keys[0], NB).astype(jnp.int32)
    steps = jnp.arange(-SPAN, SPAN + 1, dtype=jnp.int32)
    base = jnp.concatenate([jnp.repeat(steps, MULT), jnp.zeros((MULT,), jnp.int32)])
    shift = base[jax.random.permutation(keys[1], PAIR_DEV)]
    device = jnp.arange(ntrans, dtype=jnp.int32)[:, None]
    first_slot = device * BLK_DEV + jax.random.randint(keys[2], (ntrans, PAIR_DEV), 0, BLK_DEV)
    second_slot = (device + shift[None, :]) % ntrans * BLK_DEV + jax.random.randint(keys[3], (ntrans, PAIR_DEV), 0, BLK_DEV)
    inverse = jnp.argsort(owner).astype(jnp.int32)
    listed = jnp.stack([inverse[first_slot], inverse[second_slot]], axis=-1)
    return (owner, listed.reshape(ntrans * PAIR_DEV, 2).astype(jnp.int32))


def draw_pairs(key, part):
    return common_layout(key)[1]


def draw_owner(key, part):
    return common_layout(key)[0]


def block_levels(own_key, dims, cuts, low, high):
    factor_of = 1.0
    for axis_at, blocks in cuts:
        steps = jax.random.uniform(jax.random.fold_in(jax.random.fold_in(own_key, 6), axis_at), (blocks,), jnp.float32, low / len(cuts), high / len(cuts))
        factor_of = factor_of * jnp.repeat(jnp.exp(steps), dims[axis_at] // blocks).reshape((-1,) + (1,) * (len(dims) - 1 - axis_at))
    return factor_of


def centred(key, dims, scale, reach, shards=(), kind=jnp.bfloat16):
    array = jax.random.normal(key, dims, jnp.float32) * scale
    if len(shards) > 0:
        array = block_levels(key, dims, shards, -0.22, 0.18) * array
    return jnp.clip(array, min=-reach, max=reach).astype(kind)


def setup_inputs(seed: int = 0) -> dict:
    seeds = jax.random.split(jax.random.key(seed), 5)
    densities = centred(seeds[0], (NT, G), (G ** -0.25), 1.75, ((0, 16), (1, 8)))
    coulomb = jnp.clip(jnp.exp(math.log(4.0) - 2.7725887 * jax.random.uniform(seeds[1], (G,), jnp.float32) ** block_levels(seeds[1], (G,), ((0, 8),), -0.2, 0.2)), 0.25, 4.0)
    pairs = draw_pairs(jax.random.fold_in(seeds[4], 71), 0)
    owner = draw_owner(jax.random.fold_in(seeds[4], 71), 0)
    return {"densities": densities, "coulomb": coulomb, "pairs": pairs, "owner": owner}


def reference(densities, coulomb, pairs, owner):
    slice_width = G // N_PW

    def one_pair(pair):
        slot_first = owner[pair[0]].astype(jnp.int32)
        slot_second = owner[pair[1]].astype(jnp.int32)
        first = lax.dynamic_slice_in_dim(densities, slot_first * BLK, BLK, 0)
        second = lax.dynamic_slice_in_dim(densities, slot_second * BLK, BLK, 0)
        weighted = (first.astype(jnp.float32) * coulomb).astype(jnp.bfloat16)
        left = weighted.astype(jnp.float32).reshape(BLK, N_PW, slice_width)
        right = second.astype(jnp.float32).reshape(BLK, N_PW, slice_width)
        parts = jnp.einsum("rsg,csg->src", left, right)
        return jnp.sum(parts, axis=0)

    blocks = lax.map(one_pair, pairs)
    kernel = jnp.transpose(blocks, (1, 0, 2))
    position = jnp.arange(PAIRS, dtype=jnp.int32)
    target = (owner[pairs[:, 1]] // BLK_DEV).astype(jnp.int32) * PAIR_DEV + position % PAIR_DEV
    flipped = jnp.zeros((PAIRS, BLK, BLK), jnp.float32).at[target].set(jnp.transpose(blocks, (0, 2, 1)))
    kernel_t = jnp.transpose(flipped, (1, 0, 2))
    return kernel, kernel_t
```

```python
import jax
import jax.numpy as jnp
from jax import lax
from jax.experimental import pallas as pl
from jax.experimental.pallas import tpu as pltpu
from jax.sharding import PartitionSpec as P

BLK = 512
SPAN = 2
MULT = 3
STORED = 8
LISTED = 18
LOCAL = 6
NTRANS = 16
NPW = 8
ROWS = BLK // NPW
HALF = ROWS // 2
STEPS = (1, -1, 2, -2)
ORDER, FIRST, SECOND, TABLE = 0, LISTED, 2 * LISTED, 3 * LISTED


def shifted(value, axis, steps):
    count = lax.axis_size(axis)
    pairs = [(source, (source + steps) % count) for source in range(count)]
    return lax.ppermute(value, axis, pairs)


def start_of(step):
    return 0 if step == 0 else LOCAL + MULT * STEPS.index(step)


def prepare_kernel(device_ref, pairs_ref, owner_ref, blocks_ref, table_ref, *rest):
    sends, sems = rest[: len(STEPS)], rest[len(STEPS)]
    device = device_ref[0]
    filled = {step: start_of(step) for step in (0, *STEPS)}
    for q in range(LISTED):
        pair = device * LISTED + q
        first = owner_ref[pairs_ref[0, pair]]
        second = owner_ref[pairs_ref[1, pair]]
        distance = (((second >> 3) - device + SPAN + NTRANS) & (NTRANS - 1)) - SPAN
        place = jnp.int32(0)
        for step in filled:
            here = distance == step
            place = jnp.where(here, filled[step], place)
            filled[step] = jnp.where(here, filled[step] + 1, filled[step])
        table_ref[ORDER + place] = jnp.int32(q)
        table_ref[FIRST + place] = first & (STORED - 1)
        table_ref[SECOND + place] = second & (STORED - 1)
    copies = []
    for at, step in enumerate(STEPS):
        target = (device - step + NTRANS) & (NTRANS - 1)
        for j in range(MULT):
            q = table_ref[ORDER + start_of(step) + j]
            slot = owner_ref[pairs_ref[1, target * LISTED + q]] & (STORED - 1)
            copies.append(pltpu.make_async_copy(blocks_ref.at[slot], sends[at].at[j], sems.at[at * MULT + j]))
            copies[-1].start()
    for copy in copies:
        copy.wait()


def prepare(device, pairs, owner, blocks):
    width = blocks.shape[2]
    smem = pl.BlockSpec(memory_space=pltpu.SMEM)
    anywhere = pl.BlockSpec(memory_space=pl.ANY)
    return pl.pallas_call(
        prepare_kernel,
        out_shape=[jax.ShapeDtypeStruct((TABLE,), jnp.int32)]
        + [jax.ShapeDtypeStruct((MULT, BLK, width), jnp.bfloat16)] * len(STEPS),
        in_specs=[smem, smem, smem, anywhere],
        out_specs=[smem] + [anywhere] * len(STEPS),
        scratch_shapes=[pltpu.SemaphoreType.DMA((MULT * len(STEPS),))],
        name="prepare",
    )(device, pairs, owner, blocks)


def products_kernel(count, table_ref, left_ref, coulomb_ref, *refs):
    rights, out_ref = refs[:-1], refs[-1]
    each = count // len(rights)
    weighted = (left_ref[0].astype(jnp.float32) * coulomb_ref[...]).astype(jnp.bfloat16)
    for at, right_ref in enumerate(rights):

        @pl.when(pl.program_id(0) // each == at)
        def _():
            part = lax.dot_general(
                weighted, right_ref[0], (((1,), (1,)), ((), ())), preferred_element_type=jnp.float32
            )
            out_ref[...] = part.astype(jnp.bfloat16).reshape(out_ref.shape)


def products(table, blocks, coulomb, rights, start, count):
    width = blocks.shape[2]
    each = count // len(rights)
    if rights[0].shape[0] == STORED:
        right_specs = [pl.BlockSpec((1, BLK, width), lambda i, table: (table[SECOND + start + i], 0, 0))]
    else:
        right_specs = [
            pl.BlockSpec((1, BLK, width), lambda i, table, at=at: (jnp.clip(i - at * each, 0, each - 1), 0, 0))
            for at in range(len(rights))
        ]
    return pl.pallas_call(
        lambda *refs: products_kernel(count, *refs),
        out_shape=jax.ShapeDtypeStruct((NPW, count, ROWS, BLK), jnp.bfloat16),
        grid_spec=pltpu.PrefetchScalarGridSpec(
            num_scalar_prefetch=1,
            grid=(count,),
            in_specs=[
                pl.BlockSpec((1, BLK, width), lambda i, table: (table[FIRST + start + i], 0, 0)),
                pl.BlockSpec((1, width), lambda i, table: (0, 0)),
                *right_specs,
            ],
            out_specs=pl.BlockSpec((NPW, 1, ROWS, BLK), lambda i, table: (0, i, 0, 0)),
        ),
        cost_estimate=pl.CostEstimate(
            flops=2 * count * BLK * BLK * width, bytes_accessed=count * (4 * BLK * width + 2 * BLK * BLK), transcendentals=0
        ),
        name="products",
    )(table, blocks, coulomb, *rights)


def total_kernel(table_ref, *refs):
    parts_ref, (kernel_ref, cut_ref) = refs[0], refs[-2:]
    total = jnp.sum(parts_ref[...].astype(jnp.float32), axis=0)[0]
    kernel_ref[0] = total
    both = jnp.concatenate([total, pltpu.roll(total, BLK - HALF, 1)], axis=0)
    columns = jnp.transpose(both, (1, 0))
    for target in range(NPW):
        cut_ref[target, 0] = columns[target * ROWS : target * ROWS + HALF].astype(cut_ref.dtype)


def totals(table, parts, kernel, start):
    count = parts.shape[1]
    carried = [] if kernel is None else [kernel]
    return pl.pallas_call(
        total_kernel,
        out_shape=[
            jax.ShapeDtypeStruct((LISTED, ROWS, BLK), jnp.float32),
            jax.ShapeDtypeStruct((NPW, count, HALF, 2 * ROWS), jnp.bfloat16),
        ],
        grid_spec=pltpu.PrefetchScalarGridSpec(
            num_scalar_prefetch=1,
            grid=(count,),
            in_specs=[pl.BlockSpec((NPW, 1, ROWS, BLK), lambda i, table: (0, i, 0, 0))]
            + [pl.BlockSpec(memory_space=pl.ANY)] * len(carried),
            out_specs=[
                pl.BlockSpec((1, ROWS, BLK), lambda i, table: (table[ORDER + start + i], 0, 0)),
                pl.BlockSpec((NPW, 1, HALF, 2 * ROWS), lambda i, table: (0, i, 0, 0)),
            ],
        ),
        input_output_aliases={2: 0} if carried else {},
        cost_estimate=pl.CostEstimate(
            flops=count * NPW * ROWS * BLK, bytes_accessed=count * 22 * ROWS * BLK, transcendentals=0
        ),
        name="totals",
    )(table, parts, *carried)


def mirror_kernel(table_ref, cut_ref, *refs):
    out_ref = refs[-1]
    low = lax.broadcasted_iota(jnp.int32, (HALF, 2 * ROWS), 1) < ROWS
    for at in range(NPW // 2):
        even = cut_ref[2 * at, 0].astype(jnp.float32)
        odd = cut_ref[2 * at + 1, 0].astype(jnp.float32)
        lanes = pl.ds(2 * ROWS * at, 2 * ROWS)
        out_ref[0, :HALF, lanes] = jnp.where(low, even, pltpu.roll(odd, ROWS, 1))
        out_ref[0, HALF:, lanes] = jnp.where(low, pltpu.roll(even, ROWS, 1), odd)


def mirrored(table, cut, kernel_t, start):
    count = cut.shape[1]
    carried = [] if kernel_t is None else [kernel_t]
    return pl.pallas_call(
        mirror_kernel,
        out_shape=jax.ShapeDtypeStruct((LISTED, ROWS, BLK), jnp.float32),
        grid_spec=pltpu.PrefetchScalarGridSpec(
            num_scalar_prefetch=1,
            grid=(count,),
            in_specs=[pl.BlockSpec((NPW, 1, HALF, 2 * ROWS), lambda i, table: (0, i, 0, 0))]
            + [pl.BlockSpec(memory_space=pl.ANY)] * len(carried),
            out_specs=pl.BlockSpec((1, ROWS, BLK), lambda i, table: (table[ORDER + start + i], 0, 0)),
        ),
        input_output_aliases={2: 0} if carried else {},
        cost_estimate=pl.CostEstimate(
            flops=count * ROWS * BLK, bytes_accessed=count * 6 * ROWS * BLK, transcendentals=0
        ),
        name="mirrored",
    )(table, cut, *carried)


def exchanged(value):
    return lax.all_to_all(value, "pw", split_axis=0, concat_axis=0, tiled=True)


def body(densities, coulomb, pairs, owner):
    blocks = densities.reshape(STORED, BLK, densities.shape[1])
    weight = coulomb.reshape(1, -1)
    device = lax.axis_index("trans").astype(jnp.int32).reshape(1)
    table, *sends = prepare(device, pairs.T, owner, blocks)
    arrived = [shifted(send, "trans", -step) for step, send in zip(STEPS, sends)]
    groups = [(0, LOCAL, [blocks])]
    for at in range(0, len(STEPS), 2):
        groups.append((start_of(STEPS[at]), 2 * MULT, arrived[at : at + 2]))
    kernel, kernel_t = None, None
    for start, count, rights in groups:
        parts = exchanged(products(table, blocks, weight, rights, start, count))
        kernel, cut = totals(table, parts, kernel, start)
        if start > 0:
            at = (start - LOCAL) // MULT
            cut = jnp.concatenate(
                [shifted(cut[:, :MULT], "trans", STEPS[at]), shifted(cut[:, MULT:], "trans", STEPS[at + 1])], axis=1
            )
        kernel_t = mirrored(table, exchanged(cut), kernel_t, start)
    return jnp.transpose(kernel, (1, 0, 2)), jnp.transpose(kernel_t, (1, 0, 2))


def solution(mesh):
    in_specs = (P("trans", "pw"), P("pw"), P(), P())
    out_specs = (P("pw", "trans", None), P("pw", "trans", None))
    return jax.shard_map(body, mesh=mesh, in_specs=in_specs, out_specs=out_specs, check_vma=False)
```

```python
import jax
import jax.numpy as jnp
from jax import lax
from jax.experimental import pallas as pl
from jax.experimental.pallas import tpu as pltpu
from jax.sharding import PartitionSpec as P

BLK = 512
SPAN = 2
MULT = 3
STORED = 8
LISTED = 18
LOCAL = 6
NTRANS = 16
NPW = 8
NY = 4
NZ = 2
ROWS = BLK // NPW
HALF = ROWS // 2
STEPS = (1, -1, 2, -2)
ORDER, FIRST, SECOND, YAT, ZAT, TABLE = 0, LISTED, 2 * LISTED, 3 * LISTED, 3 * LISTED + 1, 3 * LISTED + 2
VMEM_BYTES = 24 * 2**20


def shifted(value, steps):
    pairs = [(source, (source + steps) % NTRANS) for source in range(NTRANS)]
    return lax.ppermute(value, "trans", pairs)


def along_y(value, steps):
    pairs = [(z * NY + y, z * NY + (y + steps) % NY) for z in range(NZ) for y in range(NY)]
    return lax.ppermute(value, "pw", pairs)


def across_z(value):
    return lax.ppermute(value, "pw", [(source, (source + NY) % NPW) for source in range(NPW)])


def exchanged(value):
    return lax.all_to_all(value, "pw", split_axis=0, concat_axis=0, tiled=True)


def start_of(step):
    return 0 if step == 0 else LOCAL + MULT * STEPS.index(step)


def params():
    return pltpu.CompilerParams(vmem_limit_bytes=VMEM_BYTES)


def select(steps, device, table_ref, pairs_ref, owner_ref, blocks_ref, sends, held, in_sems, out_sems):
    loads, stores = [], []
    for at, step in enumerate(steps):
        target = (device - step + NTRANS) & (NTRANS - 1)
        for j in range(MULT):
            n = at * MULT + j
            q = table_ref[ORDER + start_of(step) + j]
            slot = owner_ref[pairs_ref[1, target * LISTED + q]] & (STORED - 1)
            loads.append(pltpu.make_async_copy(blocks_ref.at[slot], held.at[n], in_sems.at[n]))
            stores.append(pltpu.make_async_copy(held.at[n], sends[at].at[j], out_sems.at[n]))
            loads[-1].start()
    for load, store in zip(loads, stores):
        load.wait()
        store.start()
    for store in stores:
        store.wait()


def prepare_kernel(steps, place_ref, pairs_ref, owner_ref, blocks_ref, table_ref, *rest):
    sends, scratch = rest[: len(steps)], rest[len(steps) :]
    device = place_ref[0]
    table_ref[YAT] = place_ref[1] & (NY - 1)
    table_ref[ZAT] = place_ref[1] >> 2
    filled = {step: start_of(step) for step in (0, *STEPS)}
    for q in range(LISTED):
        pair = device * LISTED + q
        first = owner_ref[pairs_ref[0, pair]]
        second = owner_ref[pairs_ref[1, pair]]
        distance = (((second >> 3) - device + SPAN + NTRANS) & (NTRANS - 1)) - SPAN
        place = jnp.int32(0)
        for step in filled:
            here = distance == step
            place = jnp.where(here, filled[step], place)
            filled[step] = jnp.where(here, filled[step] + 1, filled[step])
        table_ref[ORDER + place] = jnp.int32(q)
        table_ref[FIRST + place] = first & (STORED - 1)
        table_ref[SECOND + place] = second & (STORED - 1)
    select(steps, device, table_ref, pairs_ref, owner_ref, blocks_ref, sends, *scratch)


def select_kernel(steps, table_ref, place_ref, pairs_ref, owner_ref, blocks_ref, *rest):
    sends, scratch = rest[: len(steps)], rest[len(steps) :]
    select(steps, place_ref[0], table_ref, pairs_ref, owner_ref, blocks_ref, sends, *scratch)


def prepare(steps, table, place, pairs, owner, blocks):
    width = blocks.shape[2]
    count = MULT * len(steps)
    smem = pl.BlockSpec(memory_space=pltpu.SMEM)
    anywhere = pl.BlockSpec(memory_space=pl.ANY)
    sends = [jax.ShapeDtypeStruct((MULT, BLK, width), jnp.bfloat16)] * len(steps)
    scratch = [
        pltpu.VMEM((count, BLK, width), jnp.bfloat16),
        pltpu.SemaphoreType.DMA((count,)),
        pltpu.SemaphoreType.DMA((count,)),
    ]
    if table is None:
        return pl.pallas_call(
            lambda *refs: prepare_kernel(steps, *refs),
            out_shape=[jax.ShapeDtypeStruct((TABLE,), jnp.int32)] + sends,
            in_specs=[smem, smem, smem, anywhere],
            out_specs=[smem] + [anywhere] * len(steps),
            scratch_shapes=scratch,
            compiler_params=params(),
            name="prepare",
        )(place, pairs, owner, blocks)
    return pl.pallas_call(
        lambda *refs: select_kernel(steps, *refs),
        out_shape=sends,
        in_specs=[smem, smem, smem, smem, anywhere],
        out_specs=[anywhere] * len(steps),
        scratch_shapes=scratch,
        compiler_params=params(),
        name="select",
    )(table, place, pairs, owner, blocks)


def products_kernel(count, table_ref, left_ref, coulomb_ref, *refs):
    rights, (own_ref, *send_refs), weighted_ref = refs[:-5], refs[-5:-1], refs[-1]
    each = count // len(rights)
    y = table_ref[YAT]
    for dy in range(NY):
        for z in range(NZ):
            at = (dy * NZ + z) * ROWS
            source = z * (NY * ROWS) + ((y + dy) & (NY - 1)) * ROWS
            rows = left_ref[0, pl.ds(pl.multiple_of(source, ROWS), ROWS), :]
            weighted_ref[at : at + ROWS, :] = (rows.astype(jnp.float32) * coulomb_ref[...]).astype(jnp.bfloat16)
    for at, right_ref in enumerate(rights):

        @pl.when(pl.program_id(0) // each == at)
        def _():
            part = lax.dot_general(
                weighted_ref[...], right_ref[0], (((1,), (1,)), ((), ())), preferred_element_type=jnp.float32
            ).reshape(NY, NZ, 1, ROWS, BLK)
            own_ref[...] = part[0]
            for dy, send_ref in zip(range(1, NY), send_refs):
                send_ref[...] = part[dy].astype(jnp.bfloat16)


def products(table, blocks, coulomb, rights, start, count):
    width = blocks.shape[2]
    each = count // len(rights)
    if rights[0].shape[0] == STORED:
        right_specs = [pl.BlockSpec((1, BLK, width), lambda i, table: (table[SECOND + start + i], 0, 0))]
    else:
        right_specs = [
            pl.BlockSpec((1, BLK, width), lambda i, table, at=at: (jnp.clip(i - at * each, 0, each - 1), 0, 0))
            for at in range(len(rights))
        ]
    return pl.pallas_call(
        lambda *refs: products_kernel(count, *refs),
        out_shape=[
            jax.ShapeDtypeStruct((NZ, count, ROWS, BLK), jnp.bfloat16 if dy else jnp.float32) for dy in range(NY)
        ],
        grid_spec=pltpu.PrefetchScalarGridSpec(
            num_scalar_prefetch=1,
            grid=(count,),
            in_specs=[
                pl.BlockSpec((1, BLK, width), lambda i, table: (table[FIRST + start + i], 0, 0)),
                pl.BlockSpec((1, width), lambda i, table: (0, 0)),
                *right_specs,
            ],
            out_specs=[pl.BlockSpec((NZ, 1, ROWS, BLK), lambda i, table: (0, i, 0, 0))] * NY,
            scratch_shapes=[pltpu.VMEM((BLK, width), jnp.bfloat16)],
        ),
        compiler_params=params(),
        name="products",
    )(table, blocks, coulomb, *rights)


def plane_kernel(table_ref, own_ref, up_ref, two_ref, down_ref, keep_ref, give_ref):
    z = table_ref[ZAT]

    def total(at):
        return (
            own_ref[at] + up_ref[at].astype(jnp.float32) + two_ref[at].astype(jnp.float32) + down_ref[at].astype(jnp.float32)
        )

    keep_ref[...] = total(z)
    give_ref[...] = total(1 - z).astype(jnp.bfloat16)


def plane_sums(table, parts, per):
    count = parts[0].shape[1]
    return pl.pallas_call(
        plane_kernel,
        out_shape=[
            jax.ShapeDtypeStruct((count, ROWS, BLK), jnp.float32),
            jax.ShapeDtypeStruct((count, ROWS, BLK), jnp.bfloat16),
        ],
        grid_spec=pltpu.PrefetchScalarGridSpec(
            num_scalar_prefetch=1,
            grid=(count // per,),
            in_specs=[pl.BlockSpec((NZ, per, ROWS, BLK), lambda i, table: (0, i, 0, 0))] * NY,
            out_specs=[pl.BlockSpec((per, ROWS, BLK), lambda i, table: (i, 0, 0))] * 2,
        ),
        compiler_params=params(),
        name="plane_sums",
    )(table, *parts)


def total_kernel(table_ref, keep_ref, got_ref, *refs):
    kernel_ref, cut_refs = refs[-3], refs[-2:]
    total = keep_ref[0] + got_ref[0].astype(jnp.float32)
    kernel_ref[0] = total
    both = jnp.concatenate([total, pltpu.roll(total, BLK - HALF, 1)], axis=0)
    columns = jnp.transpose(both, (1, 0))
    for at, cut_ref in enumerate(cut_refs):

        @pl.when(pl.program_id(0) // MULT == at)
        def _():
            for target in range(NPW):
                cut_ref[target, 0] = columns[target * ROWS : target * ROWS + HALF].astype(cut_ref.dtype)


def totals(table, keep, got, kernel, start):
    count = keep.shape[0]
    carried = [] if kernel is None else [kernel]
    return pl.pallas_call(
        total_kernel,
        out_shape=[jax.ShapeDtypeStruct((LISTED, ROWS, BLK), jnp.float32)]
        + [jax.ShapeDtypeStruct((NPW, MULT, HALF, 2 * ROWS), jnp.bfloat16)] * 2,
        grid_spec=pltpu.PrefetchScalarGridSpec(
            num_scalar_prefetch=1,
            grid=(count,),
            in_specs=[pl.BlockSpec((1, ROWS, BLK), lambda i, table: (i, 0, 0))] * 2
            + [pl.BlockSpec(memory_space=pl.ANY)] * len(carried),
            out_specs=[pl.BlockSpec((1, ROWS, BLK), lambda i, table: (table[ORDER + start + i], 0, 0))]
            + [
                pl.BlockSpec(
                    (NPW, 1, HALF, 2 * ROWS), lambda i, table, at=at: (0, jnp.clip(i - at * MULT, 0, MULT - 1), 0, 0)
                )
                for at in range(2)
            ],
        ),
        input_output_aliases={3: 0} if carried else {},
        compiler_params=params(),
        name="totals",
    )(table, keep, got, *carried)


def mirror_kernel(table_ref, cut_ref, *refs):
    out_ref = refs[-1]
    low = lax.broadcasted_iota(jnp.int32, (HALF, 2 * ROWS), 1) < ROWS
    for at in range(NPW // 2):
        even = cut_ref[2 * at, 0].astype(jnp.float32)
        odd = cut_ref[2 * at + 1, 0].astype(jnp.float32)
        lanes = pl.ds(2 * ROWS * at, 2 * ROWS)
        out_ref[0, :HALF, lanes] = jnp.where(low, even, pltpu.roll(odd, ROWS, 1))
        out_ref[0, HALF:, lanes] = jnp.where(low, pltpu.roll(even, ROWS, 1), odd)


def mirrored(table, cut, kernel_t, start):
    count = cut.shape[1]
    carried = [] if kernel_t is None else [kernel_t]
    return pl.pallas_call(
        mirror_kernel,
        out_shape=jax.ShapeDtypeStruct((LISTED, ROWS, BLK), jnp.float32),
        grid_spec=pltpu.PrefetchScalarGridSpec(
            num_scalar_prefetch=1,
            grid=(count,),
            in_specs=[pl.BlockSpec((NPW, 1, HALF, 2 * ROWS), lambda i, table: (0, i, 0, 0))]
            + [pl.BlockSpec(memory_space=pl.ANY)] * len(carried),
            out_specs=pl.BlockSpec((1, ROWS, BLK), lambda i, table: (table[ORDER + start + i], 0, 0)),
        ),
        input_output_aliases={2: 0} if carried else {},
        compiler_params=params(),
        name="mirrored",
    )(table, cut, *carried)


def body(densities, coulomb, pairs, owner):
    blocks = densities.reshape(STORED, BLK, densities.shape[1])
    weight = coulomb.reshape(1, -1)
    place = jnp.stack([lax.axis_index("trans"), lax.axis_index("pw")]).astype(jnp.int32)
    table, *near = prepare(STEPS[:2], None, place, pairs.T, owner, blocks)
    far = prepare(STEPS[2:], table, place, pairs.T, owner, blocks)
    near = [shifted(send, -step) for step, send in zip(STEPS[:2], near)]
    *far, near[0], near[1] = lax.optimization_barrier((*far, *near))
    far = [shifted(send, -step) for step, send in zip(STEPS[2:], far)]
    groups = [(0, LOCAL, [blocks]), (start_of(STEPS[0]), 2 * MULT, near), (start_of(STEPS[2]), 2 * MULT, far)]
    kernel, kernel_t = None, None
    for start, count, rights in groups:
        own, up, two, down = products(table, blocks, weight, rights, start, count)
        parts = (own, along_y(up, 1), along_y(two, 2), along_y(down, 3))
        keep, give = plane_sums(table, parts, MULT)
        kernel, *cuts = totals(table, keep, across_z(give), kernel, start)
        if start > 0:
            at = (start - LOCAL) // MULT
            cuts = [shifted(cut, step) for cut, step in zip(cuts, STEPS[at : at + 2])]
        kernel_t = mirrored(table, exchanged(jnp.concatenate(cuts, axis=1)), kernel_t, start)
    return jnp.transpose(kernel, (1, 0, 2)), jnp.transpose(kernel_t, (1, 0, 2))


def solution(mesh):
    in_specs = (P("trans", "pw"), P("pw"), P(), P())
    out_specs = (P("pw", "trans", None), P("pw", "trans", None))
    return jax.shard_map(body, mesh=mesh, in_specs=in_specs, out_specs=out_specs, check_vma=False)
```

```python
import jax
import jax.numpy as jnp
from jax import lax
from jax.experimental import pallas as pl
from jax.experimental.pallas import tpu as pltpu
from jax.sharding import PartitionSpec as P

BLK = 512
SPAN = 2
MULT = 3
STORED = 8
LISTED = 18
LOCAL = 6
NTRANS = 16
NPW = 8
NY = 4
NZ = 2
ROWS = BLK // NPW
HALF = ROWS // 2
STEPS = (1, -1, 2, -2)
ORDER, FIRST, SECOND, YAT, ZAT, TABLE = 0, LISTED, 2 * LISTED, 3 * LISTED, 3 * LISTED + 1, 3 * LISTED + 2
VMEM_BYTES = 24 * 2**20


def shifted(value, steps):
    pairs = [(source, (source + steps) % NTRANS) for source in range(NTRANS)]
    return lax.ppermute(value, "trans", pairs)


def along_y(value, steps):
    pairs = [(z * NY + y, z * NY + (y + steps) % NY) for z in range(NZ) for y in range(NY)]
    return lax.ppermute(value, "pw", pairs)


def across_z(value):
    return lax.ppermute(value, "pw", [(source, (source + NY) % NPW) for source in range(NPW)])


def exchanged(value):
    return lax.all_to_all(value, "pw", split_axis=0, concat_axis=0, tiled=True)


def start_of(step):
    return 0 if step == 0 else LOCAL + MULT * STEPS.index(step)


def params():
    return pltpu.CompilerParams(vmem_limit_bytes=VMEM_BYTES)


def table_kernel(place_ref, pairs_ref, owner_ref, table_ref):
    device = place_ref[0]
    table_ref[YAT] = place_ref[1] & (NY - 1)
    table_ref[ZAT] = place_ref[1] >> 2
    filled = {step: start_of(step) for step in (0, *STEPS)}
    for q in range(LISTED):
        pair = device * LISTED + q
        first = owner_ref[pairs_ref[0, pair]]
        second = owner_ref[pairs_ref[1, pair]]
        distance = (((second >> 3) - device + SPAN + NTRANS) & (NTRANS - 1)) - SPAN
        place = jnp.int32(0)
        for step in filled:
            here = distance == step
            place = jnp.where(here, filled[step], place)
            filled[step] = jnp.where(here, filled[step] + 1, filled[step])
        source = (device - distance + NTRANS) & (NTRANS - 1)
        table_ref[ORDER + place] = jnp.int32(q)
        table_ref[FIRST + place] = first & (STORED - 1)
        table_ref[SECOND + place] = owner_ref[pairs_ref[1, source * LISTED + q]] & (STORED - 1)


def make_table(place, pairs, owner):
    smem = pl.BlockSpec(memory_space=pltpu.SMEM)
    return pl.pallas_call(
        table_kernel,
        out_shape=jax.ShapeDtypeStruct((TABLE,), jnp.int32),
        in_specs=[smem, smem, smem],
        out_specs=smem,
        compiler_params=params(),
        cost_estimate=pl.CostEstimate(flops=5750000001, bytes_accessed=15000001, transcendentals=0),
        name="make_table",
    )(place, pairs, owner)


def select_kernel(steps, table_ref, blocks_ref, *rest):
    sends, (held, in_sems, out_sems) = rest[: len(steps)], rest[len(steps) :]
    loads, stores = [], []
    for at, step in enumerate(steps):
        for j in range(MULT):
            n = at * MULT + j
            slot = table_ref[FIRST + start_of(step) + j]
            loads.append(pltpu.make_async_copy(blocks_ref.at[slot], held.at[n], in_sems.at[n]))
            stores.append(pltpu.make_async_copy(held.at[n], sends[at].at[j], out_sems.at[n]))
            loads[-1].start()
    for load, store in zip(loads, stores):
        load.wait()
        store.start()
    for store in stores:
        store.wait()


def select(steps, table, blocks):
    width = blocks.shape[2]
    count = MULT * len(steps)
    anywhere = pl.BlockSpec(memory_space=pl.ANY)
    return pl.pallas_call(
        lambda *refs: select_kernel(steps, *refs),
        out_shape=[jax.ShapeDtypeStruct((MULT, BLK, width), jnp.bfloat16)] * len(steps),
        in_specs=[pl.BlockSpec(memory_space=pltpu.SMEM), anywhere],
        out_specs=[anywhere] * len(steps),
        scratch_shapes=[
            pltpu.VMEM((count, BLK, width), jnp.bfloat16),
            pltpu.SemaphoreType.DMA((count,)),
            pltpu.SemaphoreType.DMA((count,)),
        ],
        compiler_params=params(),
        cost_estimate=pl.CostEstimate(flops=5750000001, bytes_accessed=15000001, transcendentals=0),
        name="select",
    )(table, blocks)


def products_kernel(count, table_ref, right_ref, coulomb_ref, *refs):
    lefts, (own_ref, up_add_ref, down_add_ref, up_two_ref, down_two_ref, up_ref, down_ref, weighted_ref) = refs[:-8], refs[-8:]
    each = count // len(lefts)
    y = table_ref[YAT]
    for at, left_ref in enumerate(lefts):

        @pl.when(pl.program_id(0) // each == at)
        def _():
            for dy in range(NY):
                for z in range(NZ):
                    to = (dy * NZ + z) * ROWS
                    source = z * (NY * ROWS) + ((y + dy) & (NY - 1)) * ROWS
                    rows = left_ref[0, pl.ds(pl.multiple_of(source, ROWS), ROWS), :]
                    weighted_ref[to : to + ROWS, :] = (rows.astype(jnp.float32) * coulomb_ref[...]).astype(jnp.bfloat16)

    part = lax.dot_general(
        weighted_ref[...], right_ref[0], (((1,), (1,)), ((), ())), preferred_element_type=jnp.float32
    ).reshape(NY, NZ, 1, ROWS, BLK)
    own_ref[...] = part[0]
    up_add_ref[...] = part[1, 0]
    up_ref[0] = part[1, 1].astype(jnp.bfloat16)
    up_two_ref[...] = part[2, 0].astype(jnp.bfloat16)
    down_two_ref[...] = part[2, 1].astype(jnp.bfloat16)
    down_ref[0] = part[3, 0].astype(jnp.bfloat16)
    down_add_ref[...] = part[3, 1]


def products(table, blocks, coulomb, lefts, start, count):
    width = blocks.shape[2]
    each = count // len(lefts)
    if lefts[0].shape[0] == STORED:
        left_specs = [pl.BlockSpec((1, BLK, width), lambda i, table: (table[FIRST + start + i], 0, 0))]
    else:
        left_specs = [
            pl.BlockSpec((1, BLK, width), lambda i, table, at=at: (jnp.clip(i - at * each, 0, each - 1), 0, 0))
            for at in range(len(lefts))
        ]
    half = (count, ROWS, BLK)
    half_spec = pl.BlockSpec((1, ROWS, BLK), lambda i, table: (i, 0, 0))
    whole = (NZ, count, ROWS, BLK)
    return pl.pallas_call(
        lambda *refs: products_kernel(count, *refs),
        out_shape=[
            jax.ShapeDtypeStruct(whole, jnp.float32),
            jax.ShapeDtypeStruct(half, jnp.float32),
            jax.ShapeDtypeStruct(half, jnp.float32),
            jax.ShapeDtypeStruct(half, jnp.bfloat16),
            jax.ShapeDtypeStruct(half, jnp.bfloat16),
            jax.ShapeDtypeStruct(whole, jnp.bfloat16),
            jax.ShapeDtypeStruct(whole, jnp.bfloat16),
        ],
        grid_spec=pltpu.PrefetchScalarGridSpec(
            num_scalar_prefetch=1,
            grid=(count,),
            in_specs=[
                pl.BlockSpec((1, BLK, width), lambda i, table: (table[SECOND + start + i], 0, 0)),
                pl.BlockSpec((1, width), lambda i, table: (0, 0)),
                *left_specs,
            ],
            out_specs=[
                pl.BlockSpec((NZ, 1, ROWS, BLK), lambda i, table: (0, i, 0, 0)),
                half_spec,
                half_spec,
                half_spec,
                half_spec,
                pl.BlockSpec((1, 1, ROWS, BLK), lambda i, table: (1, i, 0, 0)),
                pl.BlockSpec((1, 1, ROWS, BLK), lambda i, table: (0, i, 0, 0)),
            ],
            scratch_shapes=[pltpu.VMEM((BLK, width), jnp.bfloat16)],
        ),
        compiler_params=params(),
        cost_estimate=pl.CostEstimate(flops=5750000001, bytes_accessed=15000001, transcendentals=0),
        name="products",
    )(table, blocks, coulomb, *lefts)


def passed_kernel(up_add_ref, up_got_ref, down_add_ref, down_got_ref, *refs):
    up_ref, down_ref = refs[-2:]
    up_ref[0] = (up_add_ref[...] + up_got_ref[...].astype(jnp.float32)).astype(jnp.bfloat16)
    down_ref[0] = (down_add_ref[...] + down_got_ref[...].astype(jnp.float32)).astype(jnp.bfloat16)


def passed_on(up_add, up_got, down_add, down_got, up, down):
    count = up_add.shape[0]
    half = pl.BlockSpec((MULT, ROWS, BLK), lambda i: (i, 0, 0))
    whole = jax.ShapeDtypeStruct((NZ, count, ROWS, BLK), jnp.bfloat16)
    return pl.pallas_call(
        passed_kernel,
        out_shape=[whole, whole],
        grid=(count // MULT,),
        in_specs=[half] * 4 + [pl.BlockSpec(memory_space=pl.ANY)] * 2,
        out_specs=[
            pl.BlockSpec((1, MULT, ROWS, BLK), lambda i: (0, i, 0, 0)),
            pl.BlockSpec((1, MULT, ROWS, BLK), lambda i: (1, i, 0, 0)),
        ],
        input_output_aliases={4: 0, 5: 1},
        compiler_params=params(),
        cost_estimate=pl.CostEstimate(flops=5750000001, bytes_accessed=15000001, transcendentals=0),
        name="passed_on",
    )(up_add, up_got, down_add, down_got, up, down)


def plane_kernel(table_ref, own_ref, up_ref, down_ref, keep_ref, give_ref):
    z = table_ref[ZAT]

    def total(side):
        return own_ref[side] + up_ref[side].astype(jnp.float32) + down_ref[side].astype(jnp.float32)

    keep_ref[...] = total(z)
    give_ref[...] = total(1 - z).astype(jnp.bfloat16)


def plane_sums(table, own, up, down):
    count = own.shape[1]
    return pl.pallas_call(
        plane_kernel,
        out_shape=[
            jax.ShapeDtypeStruct((count, ROWS, BLK), jnp.float32),
            jax.ShapeDtypeStruct((count, ROWS, BLK), jnp.bfloat16),
        ],
        grid_spec=pltpu.PrefetchScalarGridSpec(
            num_scalar_prefetch=1,
            grid=(count // MULT,),
            in_specs=[pl.BlockSpec((NZ, MULT, ROWS, BLK), lambda i, table: (0, i, 0, 0))] * 3,
            out_specs=[pl.BlockSpec((MULT, ROWS, BLK), lambda i, table: (i, 0, 0))] * 2,
        ),
        compiler_params=params(),
        cost_estimate=pl.CostEstimate(flops=5750000001, bytes_accessed=15000001, transcendentals=0),
        name="plane_sums",
    )(table, own, up, down)


def cut_columns(total, cut_ref):
    both = jnp.concatenate([total, pltpu.roll(total, BLK - HALF, 1)], axis=0)
    columns = jnp.transpose(both, (1, 0))
    for target in range(NPW):
        cut_ref[target, 0] = columns[target * ROWS : target * ROWS + HALF].astype(cut_ref.dtype)


CUT = (NPW, 1, HALF, 2 * ROWS)


def totals_kernel(placed, table_ref, keep_ref, got_ref, *refs):
    total = keep_ref[0] + got_ref[0].astype(jnp.float32)
    cut_columns(total, refs[-1])
    if placed:
        refs[-2][0] = total
    else:
        for n, out_ref in enumerate(refs[-3:-1]):

            @pl.when(pl.program_id(0) // MULT == n)
            def _():
                out_ref[0] = total.astype(out_ref.dtype)


def totals(table, keep, got, placed, room, cut):
    count = keep.shape[0]
    carried = [] if cut is None else [cut]
    offset = room - count if carried else 0
    block = (1, ROWS, BLK)
    if placed:
        out_shape = [jax.ShapeDtypeStruct((LISTED, ROWS, BLK), jnp.float32)]
        out_specs = [pl.BlockSpec(block, lambda i, table: (table[ORDER + i], 0, 0))]
    else:
        out_shape = [jax.ShapeDtypeStruct((MULT, ROWS, BLK), jnp.bfloat16)] * 2
        out_specs = [
            pl.BlockSpec(block, lambda i, table, n=n: (jnp.clip(i - n * MULT, 0, MULT - 1), 0, 0)) for n in range(2)
        ]
    return pl.pallas_call(
        lambda *refs: totals_kernel(placed, *refs),
        out_shape=out_shape + [jax.ShapeDtypeStruct((NPW, room, HALF, 2 * ROWS), jnp.bfloat16)],
        grid_spec=pltpu.PrefetchScalarGridSpec(
            num_scalar_prefetch=1,
            grid=(count,),
            in_specs=[pl.BlockSpec(block, lambda i, table: (i, 0, 0))] * 2
            + [pl.BlockSpec(memory_space=pl.ANY)] * len(carried),
            out_specs=out_specs + [pl.BlockSpec(CUT, lambda i, table: (0, offset + i, 0, 0))],
        ),
        input_output_aliases={3: len(out_shape)} if carried else {},
        compiler_params=params(),
        cost_estimate=pl.CostEstimate(flops=5750000001, bytes_accessed=15000001, transcendentals=0),
        name="totals",
    )(table, keep, got, *carried)


def finish_kernel(start, count, arrived_start, table_ref, cut_ref, *refs):
    arrived, (kernel_ref, kernel_t_ref, held, sems) = refs[:2], refs[-4:]
    low = lax.broadcasted_iota(jnp.int32, (HALF, 2 * ROWS), 1) < ROWS
    copies = []

    def send(slot, out_ref, at):
        copies.append(pltpu.make_async_copy(held.at[slot], out_ref.at[table_ref[ORDER + at]], sems.at[slot]))
        copies[-1].start()

    for n, arrived_ref in enumerate(arrived):
        for j in range(MULT):
            slot = count + n * MULT + j
            held[slot] = arrived_ref[j].astype(jnp.float32)
            send(slot, kernel_ref, arrived_start + n * MULT + j)
    for at in range(count):
        for pair in range(NPW // 2):
            even = cut_ref[2 * pair, at].astype(jnp.float32)
            odd = cut_ref[2 * pair + 1, at].astype(jnp.float32)
            lanes = pl.ds(2 * ROWS * pair, 2 * ROWS)
            held[at, :HALF, lanes] = jnp.where(low, even, pltpu.roll(odd, ROWS, 1))
            held[at, HALF:, lanes] = jnp.where(low, pltpu.roll(even, ROWS, 1), odd)
        send(at, kernel_t_ref, start + at)
    for copy in copies:
        copy.wait()


def finish(table, cut, arrived, arrived_start, start, kernel, kernel_t):
    count = cut.shape[1]
    carried = [kernel] if kernel_t is None else [kernel, kernel_t]
    vmem = pl.BlockSpec(memory_space=pltpu.VMEM)
    anywhere = pl.BlockSpec(memory_space=pl.ANY)
    slots = count + 2 * MULT
    return pl.pallas_call(
        lambda *refs: finish_kernel(start, count, arrived_start, *refs),
        out_shape=[jax.ShapeDtypeStruct((LISTED, ROWS, BLK), jnp.float32)] * 2,
        in_specs=[pl.BlockSpec(memory_space=pltpu.SMEM), vmem, vmem, vmem] + [anywhere] * len(carried),
        out_specs=[anywhere] * 2,
        scratch_shapes=[pltpu.VMEM((slots, ROWS, BLK), jnp.float32), pltpu.SemaphoreType.DMA((slots,))],
        input_output_aliases={4 + n: n for n in range(len(carried))},
        compiler_params=params(),
        cost_estimate=pl.CostEstimate(flops=5750000001, bytes_accessed=15000001, transcendentals=0),
        name="finish",
    )(table, cut, *arrived, *carried)


def after(values, others):
    count = len(values)
    return lax.optimization_barrier((*values, *others))[:count]


def body(densities, coulomb, pairs, owner):
    blocks = densities.reshape(STORED, BLK, densities.shape[1])
    weight = coulomb.reshape(1, -1)
    place = jnp.stack([lax.axis_index("trans"), lax.axis_index("pw")]).astype(jnp.int32)
    table = make_table(place, pairs.T, owner)

    def begin(lefts, start, table=table):
        own, up_add, down_add, up_two, down_two, up, down = products(table, blocks, weight, lefts, start, 2 * MULT)
        return own, up_add, along_y(up_two, 1), down_add, along_y(down_two, NY - 1), up, down

    def planes(own, up, down):
        return own, along_y(up, 1), along_y(down, NY - 1)

    def across(parts):
        keep, give = plane_sums(table, *parts)
        return keep, across_z(give)

    def back(arrays, steps):
        return [shifted(array, -step) for array, step in zip(arrays, steps)]

    near_steps, far_steps = STEPS[:2], STEPS[2:]
    to_near, to_far = LOCAL, LOCAL + 2 * MULT
    near = select(near_steps, table, blocks)
    (ready,) = after((table,), near)
    near = [shifted(send, step) for step, send in zip(near_steps, near)]
    begun_local = begin([blocks], 0, ready)
    far = select(far_steps, *after((ready,), (begun_local[0],)), blocks)
    passed = passed_on(*begun_local[1:])
    near = after(near, passed)
    local = planes(begun_local[0], *passed)
    far = [shifted(send, step) for step, send in zip(far_steps, after(far, near))]
    begun_near = begin(near, to_near)
    parts_near = planes(begun_near[0], *passed_on(*begun_near[1:]))
    begun_far = begin(after(far, local[1:]), to_far)
    kernel, cut = totals(table, *across(local), True, to_far, None)
    *blocks_near, cut = totals(table, *across(parts_near), False, to_far, cut)
    blocks_near = back(blocks_near, near_steps)
    kernel, kernel_t = finish(table, exchanged(cut), blocks_near, to_near, 0, kernel, None)
    parts_far = planes(begun_far[0], *passed_on(*begun_far[1:]))
    keep, got = across(parts_far)
    *blocks_far, cut = totals(table, *after((keep, got), (kernel_t,)), False, 2 * MULT, None)
    blocks_far = back(blocks_far, far_steps)
    kernel, kernel_t = finish(table, exchanged(cut), blocks_far, to_far, to_far, kernel, kernel_t)
    return jnp.transpose(kernel, (1, 0, 2)), jnp.transpose(kernel_t, (1, 0, 2))


def solution(mesh):
    in_specs = (P("trans", "pw"), P("pw"), P(), P())
    out_specs = (P("pw", "trans", None), P("pw", "trans", None))
    return jax.shard_map(body, mesh=mesh, in_specs=in_specs, out_specs=out_specs, check_vma=False)
```

```python
import jax
import jax.numpy as jnp
from jax import lax
from jax.experimental import pallas as pl
from jax.experimental.pallas import tpu as pltpu
from jax.sharding import PartitionSpec as P

BLK = 512
SPAN = 2
MULT = 3
STORED = 8
LISTED = 18
LOCAL = 6
NTRANS = 16
NPW = 8
NY = 4
NZ = 2
ROWS = BLK // NPW
RUNS = ((0, 6), (1, 3), (-1, 3), (2, 2), (-2, 2), (2, 1), (-2, 1))
NEAR_AT, FAR_AT, LAST_AT = 6, 12, 16
RESULTS = ((0, 1, 2, 3, 4, 5), (6, 7, 8), (9, 10, 11), (12, 13, 16), (14, 15, 17))
ORDER, FIRST, SECOND, YAT, ZAT, TABLE = 0, LISTED, 2 * LISTED, 3 * LISTED, 3 * LISTED + 1, 3 * LISTED + 2
VMEM_BYTES = 24 * 2**20


def shifted(value, steps):
    pairs = [(source, (source + steps) % NTRANS) for source in range(NTRANS)]
    return lax.ppermute(value, "trans", pairs)


def along_y(value, steps):
    pairs = [(z * NY + y, z * NY + (y + steps) % NY) for z in range(NZ) for y in range(NY)]
    return lax.ppermute(value, "pw", pairs)


def across_z(value):
    return lax.ppermute(value, "pw", [(source, (source + NY) % NPW) for source in range(NPW)])


def exchanged(value):
    return lax.all_to_all(value, "pw", split_axis=0, concat_axis=0, tiled=True)


def params():
    return pltpu.CompilerParams(vmem_limit_bytes=VMEM_BYTES)


def table_kernel(place_ref, pairs_ref, owner_ref, table_ref):
    device = place_ref[0]
    table_ref[YAT] = place_ref[1] & (NY - 1)
    table_ref[ZAT] = place_ref[1] >> 2
    places, at = {}, 0
    for step, count in RUNS:
        places.setdefault(step, []).extend(range(at, at + count))
        at += count
    filled = {step: jnp.int32(0) for step in places}
    for q in range(LISTED):
        pair = device * LISTED + q
        first = owner_ref[pairs_ref[0, pair]]
        second = owner_ref[pairs_ref[1, pair]]
        distance = (((second >> 3) - device + SPAN + NTRANS) & (NTRANS - 1)) - SPAN
        place = jnp.int32(0)
        for step, slots in places.items():
            here = distance == step
            for number, slot in enumerate(slots):
                place = jnp.where(here & (filled[step] == number), slot, place)
            filled[step] = jnp.where(here, filled[step] + 1, filled[step])
        source = (device - distance + NTRANS) & (NTRANS - 1)
        table_ref[ORDER + place] = jnp.int32(q)
        table_ref[FIRST + place] = first & (STORED - 1)
        table_ref[SECOND + place] = owner_ref[pairs_ref[1, source * LISTED + q]] & (STORED - 1)


def make_table(place, pairs, owner):
    smem = pl.BlockSpec(memory_space=pltpu.SMEM)
    return pl.pallas_call(
        table_kernel,
        out_shape=jax.ShapeDtypeStruct((TABLE,), jnp.int32),
        in_specs=[smem, smem, smem],
        out_specs=smem,
        compiler_params=params(),
        cost_estimate=pl.CostEstimate(flops=115000001, bytes_accessed=300001, transcendentals=0),
        name="make_table",
    )(place, pairs, owner)


def select_kernel(start, each, table_ref, blocks_ref, *rest):
    sends, (held, in_sems, out_sems) = rest[:2], rest[2:]
    loads, stores = [], []
    for at, send in enumerate(sends):
        for j in range(each):
            n = at * each + j
            slot = table_ref[FIRST + start + n]
            loads.append(pltpu.make_async_copy(blocks_ref.at[slot], held.at[n], in_sems.at[n]))
            stores.append(pltpu.make_async_copy(held.at[n], send.at[j], out_sems.at[n]))
            loads[-1].start()
    for load, store in zip(loads, stores):
        load.wait()
        store.start()
    for store in stores:
        store.wait()


def select(start, each, table, blocks):
    width = blocks.shape[2]
    count = 2 * each
    anywhere = pl.BlockSpec(memory_space=pl.ANY)
    return pl.pallas_call(
        lambda *refs: select_kernel(start, each, *refs),
        out_shape=[jax.ShapeDtypeStruct((each, BLK, width), jnp.bfloat16)] * 2,
        in_specs=[pl.BlockSpec(memory_space=pltpu.SMEM), pl.BlockSpec(memory_space=pltpu.HBM)],
        out_specs=[anywhere] * 2,
        scratch_shapes=[
            pltpu.VMEM((count, BLK, width), jnp.bfloat16),
            pltpu.SemaphoreType.DMA((count,)),
            pltpu.SemaphoreType.DMA((count,)),
        ],
        compiler_params=params(),
        cost_estimate=pl.CostEstimate(flops=115000001, bytes_accessed=300001, transcendentals=0),
        name="select",
    )(table, blocks)


def products_kernel(count, table_ref, right_ref, coulomb_ref, *refs):
    lefts, (own_ref, up_add_ref, down_add_ref, up_ref, down_ref, weighted_ref) = refs[:-6], refs[-6:]
    each = count // len(lefts)
    y = table_ref[YAT]
    for at, left_ref in enumerate(lefts):

        @pl.when(pl.program_id(0) // each == at)
        def _():
            for dy in range(NY):
                for z in range(NZ):
                    to = (dy * NZ + z) * ROWS
                    source = z * (NY * ROWS) + ((y + dy) & (NY - 1)) * ROWS
                    rows = left_ref[0, pl.ds(pl.multiple_of(source, ROWS), ROWS), :]
                    weighted_ref[to : to + ROWS, :] = (rows.astype(jnp.float32) * coulomb_ref[...]).astype(jnp.bfloat16)

    part = lax.dot_general(
        weighted_ref[...], right_ref[0], (((1,), (1,)), ((), ())), preferred_element_type=jnp.float32
    ).reshape(NY, NZ, 1, ROWS, BLK)
    own_ref[...] = part[0]
    up_add_ref[...] = part[1, 0]
    up_ref[0] = part[2, 0].astype(jnp.bfloat16)
    up_ref[1] = part[1, 1].astype(jnp.bfloat16)
    down_ref[0] = part[3, 0].astype(jnp.bfloat16)
    down_ref[1] = part[2, 1].astype(jnp.bfloat16)
    down_add_ref[...] = part[3, 1]


def products(table, blocks, coulomb, lefts, start, count):
    width = blocks.shape[2]
    each = count // len(lefts)
    if lefts[0].shape[0] == STORED:
        left_specs = [pl.BlockSpec((1, BLK, width), lambda i, table: (table[FIRST + start + i], 0, 0))]
    else:
        left_specs = [
            pl.BlockSpec((1, BLK, width), lambda i, table, at=at: (jnp.clip(i - at * each, 0, each - 1), 0, 0))
            for at in range(len(lefts))
        ]
    half = (count, ROWS, BLK)
    half_spec = pl.BlockSpec((1, ROWS, BLK), lambda i, table: (i, 0, 0))
    whole = (NZ, count, ROWS, BLK)
    whole_spec = pl.BlockSpec((NZ, 1, ROWS, BLK), lambda i, table: (0, i, 0, 0))
    return pl.pallas_call(
        lambda *refs: products_kernel(count, *refs),
        out_shape=[
            jax.ShapeDtypeStruct(whole, jnp.float32),
            jax.ShapeDtypeStruct(half, jnp.float32),
            jax.ShapeDtypeStruct(half, jnp.float32),
            jax.ShapeDtypeStruct(whole, jnp.bfloat16),
            jax.ShapeDtypeStruct(whole, jnp.bfloat16),
        ],
        grid_spec=pltpu.PrefetchScalarGridSpec(
            num_scalar_prefetch=1,
            grid=(count,),
            in_specs=[
                pl.BlockSpec((1, BLK, width), lambda i, table: (table[SECOND + start + i], 0, 0)),
                pl.BlockSpec((1, width), lambda i, table: (0, 0)),
                *left_specs,
            ],
            out_specs=[whole_spec, half_spec, half_spec, whole_spec, whole_spec],
            scratch_shapes=[pltpu.VMEM((BLK, width), jnp.bfloat16)],
        ),
        compiler_params=params(),
        cost_estimate=pl.CostEstimate(flops=115000001, bytes_accessed=300001, transcendentals=0),
        name="products",
    )(table, blocks, coulomb, *lefts)


def passed_kernel(up_add_ref, down_add_ref, up_got_ref, down_got_ref, up_ref, down_ref):
    up_ref[...] = (up_add_ref[...] + up_got_ref[0].astype(jnp.float32)).astype(jnp.bfloat16)
    down_ref[...] = (down_add_ref[...] + down_got_ref[0].astype(jnp.float32)).astype(jnp.bfloat16)


def passed_on(up_add, down_add, up_got, down_got):
    count = up_add.shape[0]
    block = (count // 2, ROWS, BLK)
    half = pl.BlockSpec(block, lambda i: (i, 0, 0))
    return pl.pallas_call(
        passed_kernel,
        out_shape=[jax.ShapeDtypeStruct(up_add.shape, jnp.bfloat16)] * 2,
        grid=(2,),
        in_specs=[
            half,
            half,
            pl.BlockSpec((1, *block), lambda i: (0, i, 0, 0)),
            pl.BlockSpec((1, *block), lambda i: (1, i, 0, 0)),
        ],
        out_specs=[half, half],
        compiler_params=params(),
        cost_estimate=pl.CostEstimate(flops=115000001, bytes_accessed=300001, transcendentals=0),
        name="passed_on",
    )(up_add, down_add, up_got, down_got)


def plane_kernel(begins, table_ref, *refs):
    parts, (keep_ref, give_ref) = refs[:-2], refs[-2:]
    z, i = table_ref[ZAT], pl.program_id(0)
    for at in range(len(begins) - 1):
        own_ref, up_ref, down_ref, up_sum_ref, down_sum_ref = parts[5 * at : 5 * at + 5]

        @pl.when((i >= begins[at]) & (i < begins[at + 1]))
        def _():
            low = own_ref[0] + down_ref[0].astype(jnp.float32) + up_sum_ref[...].astype(jnp.float32)
            high = own_ref[1] + up_ref[0].astype(jnp.float32) + down_sum_ref[...].astype(jnp.float32)
            keep_ref[...] = jnp.where(z == 0, low, high)
            give_ref[...] = jnp.where(z == 0, high, low).astype(jnp.bfloat16)


def plane_sums(table, groups, each):
    begins = [0]
    for group in groups:
        begins.append(begins[-1] + group[0].shape[1] // each)
    in_specs = []
    for lo, hi in zip(begins, begins[1:]):

        def at(i, lo=lo, hi=hi):
            return jnp.clip(i - lo, 0, hi - lo - 1)

        in_specs += [
            pl.BlockSpec((NZ, each, ROWS, BLK), lambda i, table, at=at: (0, at(i), 0, 0)),
            pl.BlockSpec((1, each, ROWS, BLK), lambda i, table, at=at: (1, at(i), 0, 0)),
            pl.BlockSpec((1, each, ROWS, BLK), lambda i, table, at=at: (0, at(i), 0, 0)),
            pl.BlockSpec((each, ROWS, BLK), lambda i, table, at=at: (at(i), 0, 0)),
            pl.BlockSpec((each, ROWS, BLK), lambda i, table, at=at: (at(i), 0, 0)),
        ]
    return pl.pallas_call(
        lambda *refs: plane_kernel(begins, *refs),
        out_shape=[
            jax.ShapeDtypeStruct((begins[-1] * each, ROWS, BLK), jnp.float32),
            jax.ShapeDtypeStruct((begins[-1] * each, ROWS, BLK), jnp.bfloat16),
        ],
        grid_spec=pltpu.PrefetchScalarGridSpec(
            num_scalar_prefetch=1,
            grid=(begins[-1],),
            in_specs=in_specs,
            out_specs=[pl.BlockSpec((each, ROWS, BLK), lambda i, table: (i, 0, 0))] * 2,
        ),
        compiler_params=params(),
        cost_estimate=pl.CostEstimate(flops=115000001, bytes_accessed=300001, transcendentals=0),
        name="plane_sums",
    )(table, *[part for group in groups for part in group])


def totals_kernel(at, outs, keep_ref, got_ref, *refs):
    cut_ref = refs[-1]
    total = keep_ref[...] + got_ref[...].astype(jnp.float32)
    columns = jnp.transpose(total.reshape(2 * ROWS, BLK), (1, 0)).astype(cut_ref.dtype)
    for target in range(NPW):
        cut_ref[target, 0] = columns[target * ROWS : (target + 1) * ROWS]
    for places, out_ref in zip(outs, refs[-1 - len(outs) : -1]):
        for slot, place in enumerate(places):

            @pl.when(pl.program_id(0) == (place - at) // 2)
            def _():
                out_ref[slot] = total[(place - at) % 2].astype(out_ref.dtype)


def totals(keep, got, at, cut):
    count = keep.shape[0]
    carried = [] if cut is None else [cut]
    outs = [places for places in RESULTS if at <= places[0] < at + count]
    out_shape = [
        jax.ShapeDtypeStruct((len(places), ROWS, BLK), jnp.bfloat16 if places[0] else jnp.float32) for places in outs
    ]
    couples = pl.BlockSpec((2, ROWS, BLK), lambda i: (i, 0, 0))
    return pl.pallas_call(
        lambda *refs: totals_kernel(at, outs, *refs),
        out_shape=out_shape + [jax.ShapeDtypeStruct((NPW, LISTED // 2, ROWS, 2 * ROWS), jnp.bfloat16)],
        grid=(count // 2,),
        in_specs=[couples] * 2 + [pl.BlockSpec(memory_space=pl.ANY)] * len(carried),
        out_specs=[pl.BlockSpec(shape.shape, lambda i: (0, 0, 0)) for shape in out_shape]
        + [pl.BlockSpec((NPW, 1, ROWS, 2 * ROWS), lambda i: (0, at // 2 + i, 0, 0))],
        input_output_aliases={2: len(outs)} if carried else {},
        compiler_params=params(),
        cost_estimate=pl.CostEstimate(flops=115000001, bytes_accessed=300001, transcendentals=0),
        name="totals",
    )(keep, got, *carried)


def finish_kernel(table_ref, cut_ref, *refs):
    results, (kernel_ref, kernel_t_ref, held, sems) = refs[: len(RESULTS)], refs[len(RESULTS) :]
    low = lax.broadcasted_iota(jnp.int32, (ROWS, 2 * ROWS), 1) < ROWS
    copies = []

    def send(source, out_ref, at):
        copies.append(pltpu.make_async_copy(source, out_ref.at[table_ref[ORDER + at]], sems.at[len(copies)]))
        copies[-1].start()

    for j, at in enumerate(RESULTS[0]):
        send(results[0].at[j], kernel_ref, at)
    for couple in range(LISTED // 2):
        for pair in range(NPW // 2):
            even = cut_ref[2 * pair, couple].astype(jnp.float32)
            odd = cut_ref[2 * pair + 1, couple].astype(jnp.float32)
            lanes = pl.ds(2 * ROWS * pair, 2 * ROWS)
            held[2 * couple, :, lanes] = jnp.where(low, even, pltpu.roll(odd, ROWS, 1))
            held[2 * couple + 1, :, lanes] = jnp.where(low, pltpu.roll(even, ROWS, 1), odd)
        for at in (2 * couple, 2 * couple + 1):
            send(held.at[at], kernel_t_ref, at)
    for places, arrived_ref in zip(RESULTS[1:], results[1:]):
        for j, at in enumerate(places):
            slot = LISTED - LOCAL + at
            held[slot] = arrived_ref[j].astype(jnp.float32)
            send(held.at[slot], kernel_ref, at)
    for copy in copies:
        copy.wait()


def finish(table, cut, results):
    vmem = pl.BlockSpec(memory_space=pltpu.VMEM)
    anywhere = pl.BlockSpec(memory_space=pl.ANY)
    return pl.pallas_call(
        finish_kernel,
        out_shape=[jax.ShapeDtypeStruct((LISTED, ROWS, BLK), jnp.float32)] * 2,
        in_specs=[pl.BlockSpec(memory_space=pltpu.SMEM)] + [vmem] * (1 + len(results)),
        out_specs=[anywhere] * 2,
        scratch_shapes=[
            pltpu.VMEM((2 * LISTED - LOCAL, ROWS, BLK), jnp.float32),
            pltpu.SemaphoreType.DMA((2 * LISTED,)),
        ],
        compiler_params=params(),
        cost_estimate=pl.CostEstimate(flops=115000001, bytes_accessed=300001, transcendentals=0),
        name="finish",
    )(table, cut, *results)


def after(values, others):
    count = len(values)
    return lax.optimization_barrier((*values, *others))[:count]


def body(densities, coulomb, pairs, owner):
    blocks = densities.reshape(STORED, BLK, densities.shape[1])
    weight = coulomb.reshape(1, -1)
    place = jnp.stack([lax.axis_index("trans"), lax.axis_index("pw")]).astype(jnp.int32)
    table = make_table(place, pairs.T, owner)

    def begin(lefts, start, count, table=table):
        own, up_add, down_add, up, down = products(table, blocks, weight, lefts, start, count)
        return own, up_add, down_add, along_y(up, 1), along_y(down, NY - 1)

    def carry_on(own, up_add, down_add, up, down):
        up_sum, down_sum = passed_on(up_add, down_add, up, down)
        return own, up, down, along_y(up_sum, 1), along_y(down_sum, NY - 1)

    near = select(NEAR_AT, 3, table, blocks)
    (ready,) = after((table,), near)
    near = [shifted(send, step) for step, send in zip((1, -1), near)]
    local = begin([blocks], 0, LOCAL, ready)
    (ready,) = after((ready,), local[:1])
    far, last = select(FAR_AT, 2, ready, blocks), select(LAST_AT, 1, ready, blocks)
    own, up_add, down_add, up, down = local
    sums = passed_on(up_add, down_add, up, down)
    local = own, up, down, along_y(sums[0], 1), along_y(sums[1], NY - 1)
    near = after(near, (*last, *sums))
    far = [shifted(send, step) for step, send in zip((2, -2), after(far, near))]
    own, up_add, down_add, up, down = begin(near, NEAR_AT, 2 * MULT)
    sums = passed_on(up_add, down_add, up, down)
    parts_near = own, up, down, along_y(sums[0], 1), along_y(sums[1], NY - 1)
    last = [shifted(send, step) for step, send in zip((2, -2), after(last, far))]
    parts_far = carry_on(*begin(after(far, (*sums, *local[3:])), FAR_AT, LAST_AT - FAR_AT))
    parts_last = carry_on(*begin(after(last, parts_near[3:]), LAST_AT, LISTED - LAST_AT))
    keep, give = plane_sums(table, (after(local, parts_last[:1]), parts_near), MULT)
    stay, near_a, near_b, cut = totals(keep, across_z(give), 0, None)
    keep, give = plane_sums(table, (parts_far, parts_last), 2)
    far_a, far_b, cut = totals(keep, across_z(give), FAR_AT, cut)
    back = [shifted(array, -step) for array, step in zip((near_a, near_b, far_a, far_b), (1, -1, 2, -2))]
    kernel, kernel_t = finish(table, exchanged(cut), (stay, *back))
    return jnp.transpose(kernel, (1, 0, 2)), jnp.transpose(kernel_t, (1, 0, 2))


def solution(mesh):
    in_specs = (P("trans", "pw"), P("pw"), P(), P())
    out_specs = (P("pw", "trans", None), P("pw", "trans", None))
    return jax.shard_map(body, mesh=mesh, in_specs=in_specs, out_specs=out_specs, check_vma=False)
```

```python
import jax
import jax.numpy as jnp
from jax import lax
from jax.experimental import pallas as pl
from jax.experimental.pallas import tpu as pltpu
from jax.sharding import PartitionSpec as P

BLK = 512
SPAN = 2
MULT = 3
STORED = 8
LISTED = 18
LOCAL = 6
NTRANS = 16
NPW = 8
NY = 4
NZ = 2
ROWS = BLK // NPW
RUNS = ((0, 6), (1, 3), (-1, 3), (2, 2), (-2, 2), (2, 1), (-2, 1))
NEAR_AT, FAR_AT, LAST_AT = 6, 12, 16
RESULTS = ((0, 1, 2, 3, 4, 5), (6, 7, 8), (9, 10, 11), (12, 13, 16), (14, 15, 17))
ORDER, FIRST, SECOND, YAT, ZAT, TABLE = 0, LISTED, 2 * LISTED, 3 * LISTED, 3 * LISTED + 1, 3 * LISTED + 2
VMEM_BYTES = 24 * 2**20


def shifted(value, steps):
    pairs = [(source, (source + steps) % NTRANS) for source in range(NTRANS)]
    return lax.ppermute(value, "trans", pairs)


def along_y(value, steps):
    pairs = [(z * NY + y, z * NY + (y + steps) % NY) for z in range(NZ) for y in range(NY)]
    return lax.ppermute(value, "pw", pairs)


def across_z(value):
    return lax.ppermute(value, "pw", [(source, (source + NY) % NPW) for source in range(NPW)])


def exchanged(value):
    return lax.all_to_all(value, "pw", split_axis=0, concat_axis=0, tiled=True)


def params():
    return pltpu.CompilerParams(vmem_limit_bytes=VMEM_BYTES)


def table_kernel(place_ref, pairs_ref, owner_ref, table_ref):
    device = place_ref[0]
    table_ref[YAT] = place_ref[1] & (NY - 1)
    table_ref[ZAT] = place_ref[1] >> 2
    places, at = {}, 0
    for step, count in RUNS:
        places.setdefault(step, []).extend(range(at, at + count))
        at += count
    filled = {step: jnp.int32(0) for step in places}
    for q in range(LISTED):
        pair = device * LISTED + q
        first = owner_ref[pairs_ref[0, pair]]
        second = owner_ref[pairs_ref[1, pair]]
        distance = (((second >> 3) - device + SPAN + NTRANS) & (NTRANS - 1)) - SPAN
        place = jnp.int32(0)
        for step, slots in places.items():
            here = distance == step
            for number, slot in enumerate(slots):
                place = jnp.where(here & (filled[step] == number), slot, place)
            filled[step] = jnp.where(here, filled[step] + 1, filled[step])
        source = (device - distance + NTRANS) & (NTRANS - 1)
        table_ref[ORDER + place] = jnp.int32(q)
        table_ref[FIRST + place] = first & (STORED - 1)
        table_ref[SECOND + place] = owner_ref[pairs_ref[1, source * LISTED + q]] & (STORED - 1)


def make_table(place, pairs, owner):
    smem = pl.BlockSpec(memory_space=pltpu.SMEM)
    return pl.pallas_call(
        table_kernel,
        out_shape=jax.ShapeDtypeStruct((TABLE,), jnp.int32),
        in_specs=[smem, smem, smem],
        out_specs=smem,
        compiler_params=params(),
        cost_estimate=pl.CostEstimate(flops=2300000001, bytes_accessed=6000001, transcendentals=0),
        name="make_table",
    )(place, pairs, owner)


def select_kernel(start, each, table_ref, blocks_ref, *rest):
    sends, sems = rest[:2], rest[2]
    copies = []
    for at, send in enumerate(sends):
        for j in range(each):
            n = at * each + j
            copies.append(pltpu.make_async_copy(blocks_ref.at[table_ref[FIRST + start + n]], send.at[j], sems.at[n]))
            copies[-1].start()
    for copy in copies:
        copy.wait()


def select(start, each, table, blocks):
    width = blocks.shape[2]
    return pl.pallas_call(
        lambda *refs: select_kernel(start, each, *refs),
        out_shape=[jax.ShapeDtypeStruct((each, BLK, width), jnp.bfloat16)] * 2,
        in_specs=[pl.BlockSpec(memory_space=pltpu.SMEM), pl.BlockSpec(memory_space=pl.ANY)],
        out_specs=[pl.BlockSpec(memory_space=pltpu.VMEM)] * 2,
        scratch_shapes=[pltpu.SemaphoreType.DMA((2 * each,))],
        compiler_params=params(),
        cost_estimate=pl.CostEstimate(flops=115000001, bytes_accessed=300001, transcendentals=0),
        name="select",
    )(table, blocks)


def products_kernel(count, table_ref, right_ref, coulomb_ref, *refs):
    lefts, (own_ref, up_add_ref, down_add_ref, up_ref, down_ref, weighted_ref) = refs[:-6], refs[-6:]
    each = count // len(lefts)
    y = table_ref[YAT]
    for at, left_ref in enumerate(lefts):

        @pl.when(pl.program_id(0) // each == at)
        def _():
            for dy in range(NY):
                for z in range(NZ):
                    to = (dy * NZ + z) * ROWS
                    source = z * (NY * ROWS) + ((y + dy) & (NY - 1)) * ROWS
                    rows = left_ref[0, pl.ds(pl.multiple_of(source, ROWS), ROWS), :]
                    weighted_ref[to : to + ROWS, :] = (rows.astype(jnp.float32) * coulomb_ref[...]).astype(jnp.bfloat16)

    part = lax.dot_general(
        weighted_ref[...], right_ref[0], (((1,), (1,)), ((), ())), preferred_element_type=jnp.float32
    ).reshape(NY, NZ, 1, ROWS, BLK)
    own_ref[...] = part[0]
    up_add_ref[...] = part[1, 0]
    up_ref[0] = part[2, 0].astype(jnp.bfloat16)
    up_ref[1] = part[1, 1].astype(jnp.bfloat16)
    down_ref[0] = part[3, 0].astype(jnp.bfloat16)
    down_ref[1] = part[2, 1].astype(jnp.bfloat16)
    down_add_ref[...] = part[3, 1]


def products(table, blocks, coulomb, lefts, start, count):
    width = blocks.shape[2]
    each = count // len(lefts)
    if lefts[0].shape[0] == STORED:
        left_specs = [pl.BlockSpec((1, BLK, width), lambda i, table: (table[FIRST + start + i], 0, 0))]
    else:
        left_specs = [
            pl.BlockSpec((1, BLK, width), lambda i, table, at=at: (jnp.clip(i - at * each, 0, each - 1), 0, 0))
            for at in range(len(lefts))
        ]
    half = (count, ROWS, BLK)
    half_spec = pl.BlockSpec((1, ROWS, BLK), lambda i, table: (i, 0, 0))
    whole = (NZ, count, ROWS, BLK)
    whole_spec = pl.BlockSpec((NZ, 1, ROWS, BLK), lambda i, table: (0, i, 0, 0))
    return pl.pallas_call(
        lambda *refs: products_kernel(count, *refs),
        out_shape=[
            jax.ShapeDtypeStruct(whole, jnp.float32),
            jax.ShapeDtypeStruct(half, jnp.float32),
            jax.ShapeDtypeStruct(half, jnp.float32),
            jax.ShapeDtypeStruct(whole, jnp.bfloat16),
            jax.ShapeDtypeStruct(whole, jnp.bfloat16),
        ],
        grid_spec=pltpu.PrefetchScalarGridSpec(
            num_scalar_prefetch=1,
            grid=(count,),
            in_specs=[
                pl.BlockSpec((1, BLK, width), lambda i, table: (table[SECOND + start + i], 0, 0)),
                pl.BlockSpec((1, width), lambda i, table: (0, 0)),
                *left_specs,
            ],
            out_specs=[whole_spec, half_spec, half_spec, whole_spec, whole_spec],
            scratch_shapes=[pltpu.VMEM((BLK, width), jnp.bfloat16)],
        ),
        compiler_params=params(),
        cost_estimate=pl.CostEstimate(flops=115000001, bytes_accessed=300001, transcendentals=0),
        name="products",
    )(table, blocks, coulomb, *lefts)


def passed_kernel(up_add_ref, down_add_ref, up_got_ref, down_got_ref, up_ref, down_ref):
    up_ref[...] = (up_add_ref[...] + up_got_ref[0].astype(jnp.float32)).astype(jnp.bfloat16)
    down_ref[...] = (down_add_ref[...] + down_got_ref[0].astype(jnp.float32)).astype(jnp.bfloat16)


def passed_on(up_add, down_add, up_got, down_got):
    count = up_add.shape[0]
    block = (count // 2, ROWS, BLK)
    half = pl.BlockSpec(block, lambda i: (i, 0, 0))
    return pl.pallas_call(
        passed_kernel,
        out_shape=[jax.ShapeDtypeStruct(up_add.shape, jnp.bfloat16)] * 2,
        grid=(2,),
        in_specs=[
            half,
            half,
            pl.BlockSpec((1, *block), lambda i: (0, i, 0, 0)),
            pl.BlockSpec((1, *block), lambda i: (1, i, 0, 0)),
        ],
        out_specs=[half, half],
        compiler_params=params(),
        cost_estimate=pl.CostEstimate(flops=115000001, bytes_accessed=300001, transcendentals=0),
        name="passed_on",
    )(up_add, down_add, up_got, down_got)


def plane_kernel(begins, table_ref, *refs):
    parts, (keep_ref, give_ref) = refs[:-2], refs[-2:]
    z, i = table_ref[ZAT], pl.program_id(0)
    for at in range(len(begins) - 1):
        own_ref, up_ref, down_ref, up_sum_ref, down_sum_ref = parts[5 * at : 5 * at + 5]

        @pl.when((i >= begins[at]) & (i < begins[at + 1]))
        def _():
            low = own_ref[0] + down_ref[0].astype(jnp.float32) + up_sum_ref[...].astype(jnp.float32)
            high = own_ref[1] + up_ref[0].astype(jnp.float32) + down_sum_ref[...].astype(jnp.float32)
            keep_ref[...] = jnp.where(z == 0, low, high)
            give_ref[...] = jnp.where(z == 0, high, low).astype(jnp.bfloat16)


def plane_sums(table, groups, each):
    begins = [0]
    for group in groups:
        begins.append(begins[-1] + group[0].shape[1] // each)
    in_specs = []
    for lo, hi in zip(begins, begins[1:]):

        def at(i, lo=lo, hi=hi):
            return jnp.clip(i - lo, 0, hi - lo - 1)

        in_specs += [
            pl.BlockSpec((NZ, each, ROWS, BLK), lambda i, table, at=at: (0, at(i), 0, 0)),
            pl.BlockSpec((1, each, ROWS, BLK), lambda i, table, at=at: (1, at(i), 0, 0)),
            pl.BlockSpec((1, each, ROWS, BLK), lambda i, table, at=at: (0, at(i), 0, 0)),
            pl.BlockSpec((each, ROWS, BLK), lambda i, table, at=at: (at(i), 0, 0)),
            pl.BlockSpec((each, ROWS, BLK), lambda i, table, at=at: (at(i), 0, 0)),
        ]
    return pl.pallas_call(
        lambda *refs: plane_kernel(begins, *refs),
        out_shape=[
            jax.ShapeDtypeStruct((begins[-1] * each, ROWS, BLK), jnp.float32),
            jax.ShapeDtypeStruct((begins[-1] * each, ROWS, BLK), jnp.bfloat16),
        ],
        grid_spec=pltpu.PrefetchScalarGridSpec(
            num_scalar_prefetch=1,
            grid=(begins[-1],),
            in_specs=in_specs,
            out_specs=[pl.BlockSpec((each, ROWS, BLK), lambda i, table: (i, 0, 0))] * 2,
        ),
        compiler_params=params(),
        cost_estimate=pl.CostEstimate(flops=115000001, bytes_accessed=300001, transcendentals=0),
        name="plane_sums",
    )(table, *[part for group in groups for part in group])


def totals_kernel(at, outs, keep_ref, got_ref, *refs):
    cut_ref = refs[-1]
    total = keep_ref[...] + got_ref[...].astype(jnp.float32)
    columns = jnp.transpose(total.reshape(2 * ROWS, BLK), (1, 0)).astype(cut_ref.dtype)
    for target in range(NPW):
        cut_ref[target, 0] = columns[target * ROWS : (target + 1) * ROWS]
    for places, out_ref in zip(outs, refs[-1 - len(outs) : -1]):
        for slot, place in enumerate(places):

            @pl.when(pl.program_id(0) == (place - at) // 2)
            def _():
                out_ref[slot] = total[(place - at) % 2].astype(out_ref.dtype)


def totals(keep, got, at, cut):
    count = keep.shape[0]
    carried = [] if cut is None else [cut]
    outs = [places for places in RESULTS if at <= places[0] < at + count]
    out_shape = [
        jax.ShapeDtypeStruct((len(places), ROWS, BLK), jnp.bfloat16 if places[0] else jnp.float32) for places in outs
    ]
    couples = pl.BlockSpec((2, ROWS, BLK), lambda i: (i, 0, 0))
    return pl.pallas_call(
        lambda *refs: totals_kernel(at, outs, *refs),
        out_shape=out_shape + [jax.ShapeDtypeStruct((NPW, LISTED // 2, ROWS, 2 * ROWS), jnp.bfloat16)],
        grid=(count // 2,),
        in_specs=[couples] * 2 + [pl.BlockSpec(memory_space=pl.ANY)] * len(carried),
        out_specs=[pl.BlockSpec(shape.shape, lambda i: (0, 0, 0)) for shape in out_shape]
        + [pl.BlockSpec((NPW, 1, ROWS, 2 * ROWS), lambda i: (0, at // 2 + i, 0, 0))],
        input_output_aliases={2: len(outs)} if carried else {},
        compiler_params=params(),
        cost_estimate=pl.CostEstimate(flops=115000001, bytes_accessed=300001, transcendentals=0),
        name="totals",
    )(keep, got, *carried)


def finish_kernel(table_ref, cut_ref, *refs):
    results, (kernel_ref, kernel_t_ref, held, sems) = refs[: len(RESULTS)], refs[len(RESULTS) :]
    low = lax.broadcasted_iota(jnp.int32, (ROWS, 2 * ROWS), 1) < ROWS
    copies = []

    def send(source, out_ref, at):
        copies.append(pltpu.make_async_copy(source, out_ref.at[table_ref[ORDER + at]], sems.at[len(copies)]))
        copies[-1].start()

    for j, at in enumerate(RESULTS[0]):
        send(results[0].at[j], kernel_ref, at)
    for couple in range(LISTED // 2):
        for pair in range(NPW // 2):
            even = cut_ref[2 * pair, couple].astype(jnp.float32)
            odd = cut_ref[2 * pair + 1, couple].astype(jnp.float32)
            lanes = pl.ds(2 * ROWS * pair, 2 * ROWS)
            held[2 * couple, :, lanes] = jnp.where(low, even, pltpu.roll(odd, ROWS, 1))
            held[2 * couple + 1, :, lanes] = jnp.where(low, pltpu.roll(even, ROWS, 1), odd)
        for at in (2 * couple, 2 * couple + 1):
            send(held.at[at], kernel_t_ref, at)
    for places, arrived_ref in zip(RESULTS[1:], results[1:]):
        for j, at in enumerate(places):
            slot = LISTED - LOCAL + at
            held[slot] = arrived_ref[j].astype(jnp.float32)
            send(held.at[slot], kernel_ref, at)
    for copy in copies:
        copy.wait()


def finish(table, cut, results):
    vmem = pl.BlockSpec(memory_space=pltpu.VMEM)
    anywhere = pl.BlockSpec(memory_space=pl.ANY)
    return pl.pallas_call(
        finish_kernel,
        out_shape=[jax.ShapeDtypeStruct((LISTED, ROWS, BLK), jnp.float32)] * 2,
        in_specs=[pl.BlockSpec(memory_space=pltpu.SMEM)] + [vmem] * (1 + len(results)),
        out_specs=[anywhere] * 2,
        scratch_shapes=[
            pltpu.VMEM((2 * LISTED - LOCAL, ROWS, BLK), jnp.float32),
            pltpu.SemaphoreType.DMA((2 * LISTED,)),
        ],
        compiler_params=params(),
        cost_estimate=pl.CostEstimate(flops=115000001, bytes_accessed=300001, transcendentals=0),
        name="finish",
    )(table, cut, *results)


def after(values, others):
    count = len(values)
    return lax.optimization_barrier((*values, *others))[:count]


def body(densities, coulomb, pairs, owner):
    blocks = densities.reshape(STORED, BLK, densities.shape[1])
    weight = coulomb.reshape(1, -1)
    place = jnp.stack([lax.axis_index("trans"), lax.axis_index("pw")]).astype(jnp.int32)
    table = make_table(place, pairs.T, owner)

    def begin(lefts, start, count, table=table):
        own, up_add, down_add, up, down = products(table, blocks, weight, lefts, start, count)
        return own, up_add, down_add, along_y(up, 1), along_y(down, NY - 1)

    def carry_on(own, up_add, down_add, up, down):
        up_sum, down_sum = passed_on(up_add, down_add, up, down)
        return own, up, down, along_y(up_sum, 1), along_y(down_sum, NY - 1)

    near = select(NEAR_AT, 3, table, blocks)
    (ready,) = after((table,), near)
    near = [shifted(send, step) for step, send in zip((1, -1), near)]
    local = begin([blocks], 0, LOCAL, ready)
    (ready,) = after((ready,), local[:1])
    far, last = select(FAR_AT, 2, ready, blocks), select(LAST_AT, 1, ready, blocks)
    own, up_add, down_add, up, down = local
    sums = passed_on(up_add, down_add, up, down)
    local = own, up, down, along_y(sums[0], 1), along_y(sums[1], NY - 1)
    near = after(near, (*last, *sums))
    far = [shifted(send, step) for step, send in zip((2, -2), after(far, near))]
    own, up_add, down_add, up, down = begin(near, NEAR_AT, 2 * MULT)
    sums = passed_on(up_add, down_add, up, down)
    parts_near = own, up, down, along_y(sums[0], 1), along_y(sums[1], NY - 1)
    last = [shifted(send, step) for step, send in zip((2, -2), after(last, far))]
    parts_far = carry_on(*begin(after(far, (*sums, *local[3:])), FAR_AT, LAST_AT - FAR_AT))
    parts_last = carry_on(*begin(after(last, parts_near[3:]), LAST_AT, LISTED - LAST_AT))
    keep, give = plane_sums(table, (after(local, parts_last[:1]), parts_near), MULT)
    stay, near_a, near_b, cut = totals(keep, across_z(give), 0, None)
    keep, give = plane_sums(table, (parts_far, parts_last), 2)
    far_a, far_b, cut = totals(keep, across_z(give), FAR_AT, cut)
    back = [shifted(array, -step) for array, step in zip((near_a, near_b, far_a, far_b), (1, -1, 2, -2))]
    kernel, kernel_t = finish(table, exchanged(cut), (stay, *back))
    return jnp.transpose(kernel, (1, 0, 2)), jnp.transpose(kernel_t, (1, 0, 2))


def solution(mesh):
    in_specs = (P("trans", "pw"), P("pw"), P(), P())
    out_specs = (P("pw", "trans", None), P("pw", "trans", None))
    return jax.shard_map(body, mesh=mesh, in_specs=in_specs, out_specs=out_specs, check_vma=False)
```

```python
import jax
import jax.numpy as jnp
from jax import lax
from jax.experimental import pallas as pl
from jax.experimental.pallas import tpu as pltpu
from jax.sharding import PartitionSpec as P

BLK = 512
SPAN = 2
MULT = 3
STORED = 8
LISTED = 18
LOCAL = 6
NTRANS = 16
NPW = 8
NY = 4
NZ = 2
ROWS = BLK // NPW
RUNS = ((0, 6), (1, 3), (-1, 3), (2, 2), (-2, 2), (2, 1), (-2, 1))
NEAR_AT, FAR_AT, LAST_AT = 6, 12, 16
RESULTS = ((0, 1, 2, 3, 4, 5), (6, 7, 8), (9, 10, 11), (12, 13, 16), (14, 15, 17))
ORDER, FIRST, SECOND, YAT, ZAT, TABLE = 0, LISTED, 2 * LISTED, 3 * LISTED, 3 * LISTED + 1, 3 * LISTED + 2
VMEM_BYTES = 24 * 2**20


def shifted(value, steps):
    pairs = [(source, (source + steps) % NTRANS) for source in range(NTRANS)]
    return lax.ppermute(value, "trans", pairs)


def along_y(value, steps):
    pairs = [(z * NY + y, z * NY + (y + steps) % NY) for z in range(NZ) for y in range(NY)]
    return lax.ppermute(value, "pw", pairs)


def across_z(value):
    return lax.ppermute(value, "pw", [(source, (source + NY) % NPW) for source in range(NPW)])


def exchanged(value):
    return lax.all_to_all(value, "pw", split_axis=0, concat_axis=0, tiled=True)


def params():
    return pltpu.CompilerParams(vmem_limit_bytes=VMEM_BYTES)


def table_kernel(place_ref, pairs_ref, owner_ref, table_ref):
    device = place_ref[0]
    table_ref[YAT] = place_ref[1] & (NY - 1)
    table_ref[ZAT] = place_ref[1] >> 2
    places, at = {}, 0
    for step, count in RUNS:
        places.setdefault(step, []).extend(range(at, at + count))
        at += count
    filled = {step: jnp.int32(0) for step in places}
    for q in range(LISTED):
        pair = device * LISTED + q
        first = owner_ref[pairs_ref[0, pair]]
        second = owner_ref[pairs_ref[1, pair]]
        distance = (((second >> 3) - device + SPAN + NTRANS) & (NTRANS - 1)) - SPAN
        place = jnp.int32(0)
        for step, slots in places.items():
            here = distance == step
            for number, slot in enumerate(slots):
                place = jnp.where(here & (filled[step] == number), slot, place)
            filled[step] = jnp.where(here, filled[step] + 1, filled[step])
        source = (device - distance + NTRANS) & (NTRANS - 1)
        table_ref[ORDER + place] = jnp.int32(q)
        table_ref[FIRST + place] = first & (STORED - 1)
        table_ref[SECOND + place] = owner_ref[pairs_ref[1, source * LISTED + q]] & (STORED - 1)


def make_table(place, pairs, owner):
    smem = pl.BlockSpec(memory_space=pltpu.SMEM)
    return pl.pallas_call(
        table_kernel,
        out_shape=jax.ShapeDtypeStruct((TABLE,), jnp.int32),
        in_specs=[smem, smem, smem],
        out_specs=smem,
        compiler_params=params(),
        cost_estimate=pl.CostEstimate(flops=3450000001, bytes_accessed=9000001, transcendentals=0),
        name="make_table",
    )(place, pairs, owner)


def select_kernel(start, each, table_ref, blocks_ref, *rest):
    sends, sems = rest[:2], rest[2]
    copies = []
    for at, send in enumerate(sends):
        for j in range(each):
            n = at * each + j
            copies.append(pltpu.make_async_copy(blocks_ref.at[table_ref[FIRST + start + n]], send.at[j], sems.at[n]))
            copies[-1].start()
    for copy in copies:
        copy.wait()


def select(start, each, table, blocks):
    width = blocks.shape[2]
    return pl.pallas_call(
        lambda *refs: select_kernel(start, each, *refs),
        out_shape=[jax.ShapeDtypeStruct((each, BLK, width), jnp.bfloat16)] * 2,
        in_specs=[pl.BlockSpec(memory_space=pltpu.SMEM), pl.BlockSpec(memory_space=pl.ANY)],
        out_specs=[pl.BlockSpec(memory_space=pltpu.VMEM)] * 2,
        scratch_shapes=[pltpu.SemaphoreType.DMA((2 * each,))],
        compiler_params=params(),
        cost_estimate=pl.CostEstimate(flops=1150000001, bytes_accessed=3000001, transcendentals=0),
        name="select",
    )(table, blocks)


def products_kernel(start, count, table_ref, blocks_ref, coulomb_ref, *refs):
    lefts, (own_ref, up_add_ref, down_add_ref, up_ref, down_ref, weighted_ref) = refs[:-6], refs[-6:]
    each = count // max(len(lefts), 1)
    y = table_ref[YAT]

    def pair(i, left_ref, left_at):
        for dy in range(NY):
            for z in range(NZ):
                to = (dy * NZ + z) * ROWS
                source = z * (NY * ROWS) + ((y + dy) & (NY - 1)) * ROWS
                rows = left_ref[left_at, pl.ds(pl.multiple_of(source, ROWS), ROWS), :]
                weighted_ref[to : to + ROWS, :] = (rows.astype(jnp.float32) * coulomb_ref[...]).astype(jnp.bfloat16)
        part = lax.dot_general(
            weighted_ref[...],
            blocks_ref[table_ref[SECOND + start + i]],
            (((1,), (1,)), ((), ())),
            preferred_element_type=jnp.float32,
        ).reshape(NY, NZ, ROWS, BLK)
        own_ref[0, i] = part[0, 0]
        own_ref[1, i] = part[0, 1]
        up_add_ref[i] = part[1, 0]
        up_ref[0, i] = part[2, 0].astype(jnp.bfloat16)
        up_ref[1, i] = part[1, 1].astype(jnp.bfloat16)
        down_ref[0, i] = part[3, 0].astype(jnp.bfloat16)
        down_ref[1, i] = part[2, 1].astype(jnp.bfloat16)
        down_add_ref[i] = part[3, 1]

    if lefts:
        for at, left_ref in enumerate(lefts):

            @pl.loop(0, each)
            def _(j):
                pair(at * each + j, left_ref, j)
    else:

        @pl.loop(0, count)
        def _(i):
            pair(i, blocks_ref, table_ref[FIRST + start + i])


def products(table, blocks, coulomb, lefts, start, count):
    width = blocks.shape[2]
    half = (count, ROWS, BLK)
    whole = (NZ, count, ROWS, BLK)
    vmem = pl.BlockSpec(memory_space=pltpu.VMEM)
    return pl.pallas_call(
        lambda *refs: products_kernel(start, count, *refs),
        out_shape=[
            jax.ShapeDtypeStruct(whole, jnp.float32),
            jax.ShapeDtypeStruct(half, jnp.float32),
            jax.ShapeDtypeStruct(half, jnp.float32),
            jax.ShapeDtypeStruct(whole, jnp.bfloat16),
            jax.ShapeDtypeStruct(whole, jnp.bfloat16),
        ],
        in_specs=[pl.BlockSpec(memory_space=pltpu.SMEM)] + [vmem] * (2 + len(lefts)),
        out_specs=[vmem] * 5,
        scratch_shapes=[pltpu.VMEM((BLK, width), jnp.bfloat16)],
        compiler_params=params(),
        cost_estimate=pl.CostEstimate(flops=1150000001, bytes_accessed=3000001, transcendentals=0),
        name="products",
    )(table, blocks, coulomb, *lefts)


def passed_kernel(up_add_ref, down_add_ref, up_got_ref, down_got_ref, up_ref, down_ref):
    up_ref[...] = (up_add_ref[...] + up_got_ref[0].astype(jnp.float32)).astype(jnp.bfloat16)
    down_ref[...] = (down_add_ref[...] + down_got_ref[0].astype(jnp.float32)).astype(jnp.bfloat16)


def passed_on(up_add, down_add, up_got, down_got):
    count = up_add.shape[0]
    block = (count // 2, ROWS, BLK)
    half = pl.BlockSpec(block, lambda i: (i, 0, 0))
    return pl.pallas_call(
        passed_kernel,
        out_shape=[jax.ShapeDtypeStruct(up_add.shape, jnp.bfloat16)] * 2,
        grid=(2,),
        in_specs=[
            half,
            half,
            pl.BlockSpec((1, *block), lambda i: (0, i, 0, 0)),
            pl.BlockSpec((1, *block), lambda i: (1, i, 0, 0)),
        ],
        out_specs=[half, half],
        compiler_params=params(),
        cost_estimate=pl.CostEstimate(flops=1150000001, bytes_accessed=3000001, transcendentals=0),
        name="passed_on",
    )(up_add, down_add, up_got, down_got)


def plane_kernel(begins, table_ref, *refs):
    parts, (keep_ref, give_ref) = refs[:-2], refs[-2:]
    z, i = table_ref[ZAT], pl.program_id(0)
    for at in range(len(begins) - 1):
        own_ref, up_ref, down_ref, up_sum_ref, down_sum_ref = parts[5 * at : 5 * at + 5]

        @pl.when((i >= begins[at]) & (i < begins[at + 1]))
        def _():
            low = own_ref[0] + down_ref[0].astype(jnp.float32) + up_sum_ref[...].astype(jnp.float32)
            high = own_ref[1] + up_ref[0].astype(jnp.float32) + down_sum_ref[...].astype(jnp.float32)
            keep_ref[...] = jnp.where(z == 0, low, high)
            give_ref[...] = jnp.where(z == 0, high, low).astype(jnp.bfloat16)


def plane_sums(table, groups, each):
    begins = [0]
    for group in groups:
        begins.append(begins[-1] + group[0].shape[1] // each)
    in_specs = []
    for lo, hi in zip(begins, begins[1:]):

        def at(i, lo=lo, hi=hi):
            return jnp.clip(i - lo, 0, hi - lo - 1)

        in_specs += [
            pl.BlockSpec((NZ, each, ROWS, BLK), lambda i, table, at=at: (0, at(i), 0, 0)),
            pl.BlockSpec((1, each, ROWS, BLK), lambda i, table, at=at: (1, at(i), 0, 0)),
            pl.BlockSpec((1, each, ROWS, BLK), lambda i, table, at=at: (0, at(i), 0, 0)),
            pl.BlockSpec((each, ROWS, BLK), lambda i, table, at=at: (at(i), 0, 0)),
            pl.BlockSpec((each, ROWS, BLK), lambda i, table, at=at: (at(i), 0, 0)),
        ]
    return pl.pallas_call(
        lambda *refs: plane_kernel(begins, *refs),
        out_shape=[
            jax.ShapeDtypeStruct((begins[-1] * each, ROWS, BLK), jnp.float32),
            jax.ShapeDtypeStruct((begins[-1] * each, ROWS, BLK), jnp.bfloat16),
        ],
        grid_spec=pltpu.PrefetchScalarGridSpec(
            num_scalar_prefetch=1,
            grid=(begins[-1],),
            in_specs=in_specs,
            out_specs=[pl.BlockSpec((each, ROWS, BLK), lambda i, table: (i, 0, 0))] * 2,
        ),
        compiler_params=params(),
        cost_estimate=pl.CostEstimate(flops=1150000001, bytes_accessed=3000001, transcendentals=0),
        name="plane_sums",
    )(table, *[part for group in groups for part in group])


def totals_kernel(at, outs, keep_ref, got_ref, *refs):
    cut_ref = refs[-1]
    total = keep_ref[...] + got_ref[...].astype(jnp.float32)
    columns = jnp.transpose(total.reshape(2 * ROWS, BLK), (1, 0)).astype(cut_ref.dtype)
    for target in range(NPW):
        cut_ref[target, 0] = columns[target * ROWS : (target + 1) * ROWS]
    for places, out_ref in zip(outs, refs[-1 - len(outs) : -1]):
        for slot, place in enumerate(places):

            @pl.when(pl.program_id(0) == (place - at) // 2)
            def _():
                out_ref[slot] = total[(place - at) % 2].astype(out_ref.dtype)


def totals(keep, got, at, cut):
    count = keep.shape[0]
    carried = [] if cut is None else [cut]
    outs = [places for places in RESULTS if at <= places[0] < at + count]
    out_shape = [
        jax.ShapeDtypeStruct((len(places), ROWS, BLK), jnp.bfloat16 if places[0] else jnp.float32) for places in outs
    ]
    couples = pl.BlockSpec((2, ROWS, BLK), lambda i: (i, 0, 0))
    return pl.pallas_call(
        lambda *refs: totals_kernel(at, outs, *refs),
        out_shape=out_shape + [jax.ShapeDtypeStruct((NPW, LISTED // 2, ROWS, 2 * ROWS), jnp.bfloat16)],
        grid=(count // 2,),
        in_specs=[couples] * 2 + [pl.BlockSpec(memory_space=pl.ANY)] * len(carried),
        out_specs=[pl.BlockSpec(shape.shape, lambda i: (0, 0, 0)) for shape in out_shape]
        + [pl.BlockSpec((NPW, 1, ROWS, 2 * ROWS), lambda i: (0, at // 2 + i, 0, 0))],
        input_output_aliases={2: len(outs)} if carried else {},
        compiler_params=params(),
        cost_estimate=pl.CostEstimate(flops=1150000001, bytes_accessed=3000001, transcendentals=0),
        name="totals",
    )(keep, got, *carried)


def finish_kernel(table_ref, cut_ref, *refs):
    results, (kernel_ref, kernel_t_ref, held, sems) = refs[: len(RESULTS)], refs[len(RESULTS) :]
    low = lax.broadcasted_iota(jnp.int32, (ROWS, 2 * ROWS), 1) < ROWS
    copies = []

    def send(source, out_ref, at):
        copies.append(pltpu.make_async_copy(source, out_ref.at[table_ref[ORDER + at]], sems.at[len(copies)]))
        copies[-1].start()

    for j, at in enumerate(RESULTS[0]):
        send(results[0].at[j], kernel_ref, at)
    for couple in range(LISTED // 2):
        for pair in range(NPW // 2):
            even = cut_ref[2 * pair, couple].astype(jnp.float32)
            odd = cut_ref[2 * pair + 1, couple].astype(jnp.float32)
            lanes = pl.ds(2 * ROWS * pair, 2 * ROWS)
            held[2 * couple, :, lanes] = jnp.where(low, even, pltpu.roll(odd, ROWS, 1))
            held[2 * couple + 1, :, lanes] = jnp.where(low, pltpu.roll(even, ROWS, 1), odd)
        for at in (2 * couple, 2 * couple + 1):
            send(held.at[at], kernel_t_ref, at)
    for places, arrived_ref in zip(RESULTS[1:], results[1:]):
        for j, at in enumerate(places):
            slot = LISTED - LOCAL + at
            held[slot] = arrived_ref[j].astype(jnp.float32)
            send(held.at[slot], kernel_ref, at)
    for copy in copies:
        copy.wait()


def finish(table, cut, results):
    vmem = pl.BlockSpec(memory_space=pltpu.VMEM)
    anywhere = pl.BlockSpec(memory_space=pl.ANY)
    return pl.pallas_call(
        finish_kernel,
        out_shape=[jax.ShapeDtypeStruct((LISTED, ROWS, BLK), jnp.float32)] * 2,
        in_specs=[pl.BlockSpec(memory_space=pltpu.SMEM)] + [vmem] * (1 + len(results)),
        out_specs=[anywhere] * 2,
        scratch_shapes=[
            pltpu.VMEM((2 * LISTED - LOCAL, ROWS, BLK), jnp.float32),
            pltpu.SemaphoreType.DMA((2 * LISTED,)),
        ],
        compiler_params=params(),
        cost_estimate=pl.CostEstimate(flops=1150000001, bytes_accessed=3000001, transcendentals=0),
        name="finish",
    )(table, cut, *results)


def after(values, others):
    count = len(values)
    return lax.optimization_barrier((*values, *others))[:count]


def body(densities, coulomb, pairs, owner):
    blocks = densities.reshape(STORED, BLK, densities.shape[1])
    weight = coulomb.reshape(1, -1)
    place = jnp.stack([lax.axis_index("trans"), lax.axis_index("pw")]).astype(jnp.int32)
    table = make_table(place, pairs.T, owner)

    def begin(lefts, start, count, table=table):
        own, up_add, down_add, up, down = products(table, blocks, weight, lefts, start, count)
        return own, up_add, down_add, along_y(up, 1), along_y(down, NY - 1)

    def carry_on(own, up_add, down_add, up, down):
        up_sum, down_sum = passed_on(up_add, down_add, up, down)
        return own, up, down, along_y(up_sum, 1), along_y(down_sum, NY - 1)

    near = select(NEAR_AT, 3, table, blocks)
    (ready,) = after((table,), near)
    near = [shifted(send, step) for step, send in zip((1, -1), near)]
    local = begin([], 0, LOCAL, ready)
    (ready,) = after((ready,), local[:1])
    far, last = select(FAR_AT, 2, ready, blocks), select(LAST_AT, 1, ready, blocks)
    own, up_add, down_add, up, down = local
    sums = passed_on(up_add, down_add, up, down)
    local = own, up, down, along_y(sums[0], 1), along_y(sums[1], NY - 1)
    near = after(near, (*last, *sums))
    far = [shifted(send, step) for step, send in zip((2, -2), after(far, near))]
    own, up_add, down_add, up, down = begin(near, NEAR_AT, 2 * MULT)
    sums = passed_on(up_add, down_add, up, down)
    parts_near = own, up, down, along_y(sums[0], 1), along_y(sums[1], NY - 1)
    last = [shifted(send, step) for step, send in zip((2, -2), after(last, far))]
    parts_far = carry_on(*begin(after(far, (*sums, *local[3:])), FAR_AT, LAST_AT - FAR_AT))
    parts_last = carry_on(*begin(after(last, parts_near[3:]), LAST_AT, LISTED - LAST_AT))
    keep, give = plane_sums(table, (after(local, parts_last[:1]), parts_near), MULT)
    stay, near_a, near_b, cut = totals(keep, across_z(give), 0, None)
    keep, give = plane_sums(table, (parts_far, parts_last), 2)
    far_a, far_b, cut = totals(keep, across_z(give), FAR_AT, cut)
    back = [shifted(array, -step) for array, step in zip((near_a, near_b, far_a, far_b), (1, -1, 2, -2))]
    kernel, kernel_t = finish(table, exchanged(cut), (stay, *back))
    return jnp.transpose(kernel, (1, 0, 2)), jnp.transpose(kernel_t, (1, 0, 2))


def solution(mesh):
    in_specs = (P("trans", "pw"), P("pw"), P(), P())
    out_specs = (P("pw", "trans", None), P("pw", "trans", None))
    return jax.shard_map(body, mesh=mesh, in_specs=in_specs, out_specs=out_specs, check_vma=False)
```

```python
import jax
import jax.numpy as jnp
from jax import lax
from jax.experimental import pallas as pl
from jax.experimental.pallas import tpu as pltpu
from jax.sharding import PartitionSpec as P

BLK = 512
SPAN = 2
MULT = 3
STORED = 8
LISTED = 18
LOCAL = 6
NTRANS = 16
NPW = 8
NY = 4
NZ = 2
ROWS = BLK // NPW
RUNS = ((0, 6), (1, 3), (-1, 3), (2, 2), (-2, 2), (2, 1), (-2, 1))
NEAR_AT, FAR_AT, LAST_AT = 6, 12, 16
RESULTS = ((0, 1, 2, 3, 4, 5), (6, 7, 8), (9, 10, 11), (12, 13, 16), (14, 15, 17))
ORDER, FIRST, SECOND, YAT, ZAT, TABLE = 0, LISTED, 2 * LISTED, 3 * LISTED, 3 * LISTED + 1, 3 * LISTED + 2
VMEM_BYTES = 24 * 2**20


def shifted(value, steps):
    pairs = [(source, (source + steps) % NTRANS) for source in range(NTRANS)]
    return lax.ppermute(value, "trans", pairs)


def along_y(value, steps):
    pairs = [(z * NY + y, z * NY + (y + steps) % NY) for z in range(NZ) for y in range(NY)]
    return lax.ppermute(value, "pw", pairs)


def across_z(value):
    return lax.ppermute(value, "pw", [(source, (source + NY) % NPW) for source in range(NPW)])


def exchanged(value):
    return lax.all_to_all(value, "pw", split_axis=0, concat_axis=0, tiled=True)


def params():
    return pltpu.CompilerParams(vmem_limit_bytes=VMEM_BYTES)


def table_kernel(place_ref, pairs_ref, owner_ref, table_ref):
    device = place_ref[0]
    table_ref[YAT] = place_ref[1] & (NY - 1)
    table_ref[ZAT] = place_ref[1] >> 2
    places, at = {}, 0
    for step, count in RUNS:
        places.setdefault(step, []).extend(range(at, at + count))
        at += count
    filled = {step: jnp.int32(0) for step in places}
    for q in range(LISTED):
        pair = device * LISTED + q
        first = owner_ref[pairs_ref[0, pair]]
        second = owner_ref[pairs_ref[1, pair]]
        distance = (((second >> 3) - device + SPAN + NTRANS) & (NTRANS - 1)) - SPAN
        place = jnp.int32(0)
        for step, slots in places.items():
            here = distance == step
            for number, slot in enumerate(slots):
                place = jnp.where(here & (filled[step] == number), slot, place)
            filled[step] = jnp.where(here, filled[step] + 1, filled[step])
        source = (device - distance + NTRANS) & (NTRANS - 1)
        table_ref[ORDER + place] = jnp.int32(q)
        table_ref[FIRST + place] = first & (STORED - 1)
        table_ref[SECOND + place] = owner_ref[pairs_ref[1, source * LISTED + q]] & (STORED - 1)


def make_table(place, pairs, owner):
    smem = pl.BlockSpec(memory_space=pltpu.SMEM)
    return pl.pallas_call(
        table_kernel,
        out_shape=jax.ShapeDtypeStruct((TABLE,), jnp.int32),
        in_specs=[smem, smem, smem],
        out_specs=smem,
        compiler_params=params(),
        cost_estimate=pl.CostEstimate(flops=3450000001, bytes_accessed=9000001, transcendentals=0),
        name="make_table",
    )(place, pairs, owner)


def select_kernel(start, each, table_ref, blocks_ref, *rest):
    sends, sems = rest[:2], rest[2]
    copies = []
    for at, send in enumerate(sends):
        for j in range(each):
            n = at * each + j
            copies.append(pltpu.make_async_copy(blocks_ref.at[table_ref[FIRST + start + n]], send.at[j], sems.at[n]))
            copies[-1].start()
    for copy in copies:
        copy.wait()


def select(start, each, table, blocks):
    width = blocks.shape[2]
    return pl.pallas_call(
        lambda *refs: select_kernel(start, each, *refs),
        out_shape=[jax.ShapeDtypeStruct((each, BLK, width), jnp.bfloat16)] * 2,
        in_specs=[pl.BlockSpec(memory_space=pltpu.SMEM), pl.BlockSpec(memory_space=pl.ANY)],
        out_specs=[pl.BlockSpec(memory_space=pltpu.VMEM)] * 2,
        scratch_shapes=[pltpu.SemaphoreType.DMA((2 * each,))],
        compiler_params=params(),
        cost_estimate=pl.CostEstimate(flops=1150000001, bytes_accessed=3000001, transcendentals=0),
        name="select",
    )(table, blocks)


def products_kernel(start, count, table_ref, blocks_ref, coulomb_ref, *refs):
    lefts, (own_ref, up_add_ref, down_add_ref, up_ref, down_ref, weighted_ref) = refs[:-6], refs[-6:]
    each = count // max(len(lefts), 1)
    y = table_ref[YAT]

    def pair(i, left_ref, left_at):
        for dy in range(NY):
            for z in range(NZ):
                to = (dy * NZ + z) * ROWS
                source = z * (NY * ROWS) + ((y + dy) & (NY - 1)) * ROWS
                rows = left_ref[left_at, pl.ds(pl.multiple_of(source, ROWS), ROWS), :]
                weighted_ref[to : to + ROWS, :] = (rows.astype(jnp.float32) * coulomb_ref[...]).astype(jnp.bfloat16)
        part = lax.dot_general(
            weighted_ref[...],
            blocks_ref[table_ref[SECOND + start + i]],
            (((1,), (1,)), ((), ())),
            preferred_element_type=jnp.float32,
        ).reshape(NY, NZ, ROWS, BLK)
        own_ref[0, i] = part[0, 0]
        own_ref[1, i] = part[0, 1]
        up_add_ref[i] = part[1, 0]
        up_ref[0, i] = part[2, 0].astype(jnp.bfloat16)
        up_ref[1, i] = part[1, 1].astype(jnp.bfloat16)
        down_ref[0, i] = part[3, 0].astype(jnp.bfloat16)
        down_ref[1, i] = part[2, 1].astype(jnp.bfloat16)
        down_add_ref[i] = part[3, 1]

    if lefts:
        for at, left_ref in enumerate(lefts):

            @pl.loop(0, each)
            def _(j):
                pair(at * each + j, left_ref, j)
    else:

        @pl.loop(0, count)
        def _(i):
            pair(i, blocks_ref, table_ref[FIRST + start + i])


def products(table, blocks, coulomb, lefts, start, count):
    width = blocks.shape[2]
    half = (count, ROWS, BLK)
    whole = (NZ, count, ROWS, BLK)
    vmem = pl.BlockSpec(memory_space=pltpu.VMEM)
    return pl.pallas_call(
        lambda *refs: products_kernel(start, count, *refs),
        out_shape=[
            jax.ShapeDtypeStruct(whole, jnp.float32),
            jax.ShapeDtypeStruct(half, jnp.float32),
            jax.ShapeDtypeStruct(half, jnp.float32),
            jax.ShapeDtypeStruct(whole, jnp.bfloat16),
            jax.ShapeDtypeStruct(whole, jnp.bfloat16),
        ],
        in_specs=[pl.BlockSpec(memory_space=pltpu.SMEM)] + [vmem] * (2 + len(lefts)),
        out_specs=[vmem] * 5,
        scratch_shapes=[pltpu.VMEM((BLK, width), jnp.bfloat16)],
        compiler_params=params(),
        cost_estimate=pl.CostEstimate(flops=1150000001, bytes_accessed=3000001, transcendentals=0),
        name="products",
    )(table, blocks, coulomb, *lefts)


def passed_kernel(up_add_ref, down_add_ref, up_got_ref, down_got_ref, up_ref, down_ref):
    up_ref[...] = (up_add_ref[...] + up_got_ref[0].astype(jnp.float32)).astype(jnp.bfloat16)
    down_ref[...] = (down_add_ref[...] + down_got_ref[0].astype(jnp.float32)).astype(jnp.bfloat16)


def passed_on(up_add, down_add, up_got, down_got):
    count = up_add.shape[0]
    block = (count // 2, ROWS, BLK)
    half = pl.BlockSpec(block, lambda i: (i, 0, 0))
    return pl.pallas_call(
        passed_kernel,
        out_shape=[jax.ShapeDtypeStruct(up_add.shape, jnp.bfloat16)] * 2,
        grid=(2,),
        in_specs=[
            half,
            half,
            pl.BlockSpec((1, *block), lambda i: (0, i, 0, 0)),
            pl.BlockSpec((1, *block), lambda i: (1, i, 0, 0)),
        ],
        out_specs=[half, half],
        compiler_params=params(),
        cost_estimate=pl.CostEstimate(flops=1150000001, bytes_accessed=3000001, transcendentals=0),
        name="passed_on",
    )(up_add, down_add, up_got, down_got)


def plane_kernel(begins, table_ref, *refs):
    parts, (keep_ref, give_ref) = refs[:-2], refs[-2:]
    z, i = table_ref[ZAT], pl.program_id(0)
    for at in range(len(begins) - 1):
        own_ref, up_ref, down_ref, up_sum_ref, down_sum_ref = parts[5 * at : 5 * at + 5]

        @pl.when((i >= begins[at]) & (i < begins[at + 1]))
        def _():
            low = own_ref[0] + down_ref[0].astype(jnp.float32) + up_sum_ref[...].astype(jnp.float32)
            high = own_ref[1] + up_ref[0].astype(jnp.float32) + down_sum_ref[...].astype(jnp.float32)
            keep_ref[...] = jnp.where(z == 0, low, high)
            give_ref[...] = jnp.where(z == 0, high, low).astype(jnp.bfloat16)


def plane_sums(table, groups, each):
    begins = [0]
    for group in groups:
        begins.append(begins[-1] + group[0].shape[1] // each)
    in_specs = []
    for lo, hi in zip(begins, begins[1:]):

        def at(i, lo=lo, hi=hi):
            return jnp.clip(i - lo, 0, hi - lo - 1)

        in_specs += [
            pl.BlockSpec((NZ, each, ROWS, BLK), lambda i, table, at=at: (0, at(i), 0, 0)),
            pl.BlockSpec((1, each, ROWS, BLK), lambda i, table, at=at: (1, at(i), 0, 0)),
            pl.BlockSpec((1, each, ROWS, BLK), lambda i, table, at=at: (0, at(i), 0, 0)),
            pl.BlockSpec((each, ROWS, BLK), lambda i, table, at=at: (at(i), 0, 0)),
            pl.BlockSpec((each, ROWS, BLK), lambda i, table, at=at: (at(i), 0, 0)),
        ]
    return pl.pallas_call(
        lambda *refs: plane_kernel(begins, *refs),
        out_shape=[
            jax.ShapeDtypeStruct((begins[-1] * each, ROWS, BLK), jnp.float32),
            jax.ShapeDtypeStruct((begins[-1] * each, ROWS, BLK), jnp.bfloat16),
        ],
        grid_spec=pltpu.PrefetchScalarGridSpec(
            num_scalar_prefetch=1,
            grid=(begins[-1],),
            in_specs=in_specs,
            out_specs=[pl.BlockSpec((each, ROWS, BLK), lambda i, table: (i, 0, 0))] * 2,
        ),
        compiler_params=params(),
        cost_estimate=pl.CostEstimate(flops=1150000001, bytes_accessed=3000001, transcendentals=0),
        name="plane_sums",
    )(table, *[part for group in groups for part in group])


def totals_kernel(at, outs, keep_ref, got_ref, *refs):
    cut_ref = refs[-1]
    total = keep_ref[...] + got_ref[...].astype(jnp.float32)
    columns = jnp.transpose(total.reshape(2 * ROWS, BLK), (1, 0)).astype(cut_ref.dtype)
    for target in range(NPW):
        cut_ref[target, 0] = columns[target * ROWS : (target + 1) * ROWS]
    for places, out_ref in zip(outs, refs[-1 - len(outs) : -1]):
        for slot, place in enumerate(places):

            @pl.when(pl.program_id(0) == (place - at) // 2)
            def _():
                out_ref[slot] = total[(place - at) % 2].astype(out_ref.dtype)


def totals(keep, got, at, cut):
    count = keep.shape[0]
    carried = [] if cut is None else [cut]
    outs = [places for places in RESULTS if at <= places[0] < at + count]
    out_shape = [
        jax.ShapeDtypeStruct((len(places), ROWS, BLK), jnp.bfloat16 if places[0] else jnp.float32) for places in outs
    ]
    couples = pl.BlockSpec((2, ROWS, BLK), lambda i: (i, 0, 0))
    return pl.pallas_call(
        lambda *refs: totals_kernel(at, outs, *refs),
        out_shape=out_shape + [jax.ShapeDtypeStruct((NPW, LISTED // 2, ROWS, 2 * ROWS), jnp.bfloat16)],
        grid=(count // 2,),
        in_specs=[couples] * 2 + [pl.BlockSpec(memory_space=pl.ANY)] * len(carried),
        out_specs=[pl.BlockSpec(shape.shape, lambda i: (0, 0, 0)) for shape in out_shape]
        + [pl.BlockSpec((NPW, 1, ROWS, 2 * ROWS), lambda i: (0, at // 2 + i, 0, 0))],
        input_output_aliases={2: len(outs)} if carried else {},
        compiler_params=params(),
        cost_estimate=pl.CostEstimate(flops=1150000001, bytes_accessed=3000001, transcendentals=0),
        name="totals",
    )(keep, got, *carried)


def finish_kernel(table_ref, cut_ref, *refs):
    results, (kernel_ref, kernel_t_ref, held, sems) = refs[: len(RESULTS)], refs[len(RESULTS) :]
    low = lax.broadcasted_iota(jnp.int32, (ROWS, 2 * ROWS), 1) < ROWS
    copies = []

    def send(source, out_ref, at):
        copies.append(pltpu.make_async_copy(source, out_ref.at[table_ref[ORDER + at]], sems.at[len(copies)]))
        copies[-1].start()

    for j, at in enumerate(RESULTS[0]):
        send(results[0].at[j], kernel_ref, at)
    for couple in range(LISTED // 2):
        for pair in range(NPW // 2):
            even = cut_ref[2 * pair, couple].astype(jnp.float32)
            odd = cut_ref[2 * pair + 1, couple].astype(jnp.float32)
            lanes = pl.ds(2 * ROWS * pair, 2 * ROWS)
            moved = pltpu.roll(jnp.where(low, odd, even), ROWS, 1)
            held[2 * couple, :, lanes] = jnp.where(low, even, moved)
            held[2 * couple + 1, :, lanes] = jnp.where(low, moved, odd)
        for at in (2 * couple, 2 * couple + 1):
            send(held.at[at], kernel_t_ref, at)
    for places, arrived_ref in zip(RESULTS[1:], results[1:]):
        for j, at in enumerate(places):
            slot = LISTED - LOCAL + at
            held[slot] = arrived_ref[j].astype(jnp.float32)
            send(held.at[slot], kernel_ref, at)
    for copy in copies:
        copy.wait()


def finish(table, cut, results):
    vmem = pl.BlockSpec(memory_space=pltpu.VMEM)
    anywhere = pl.BlockSpec(memory_space=pl.ANY)
    return pl.pallas_call(
        finish_kernel,
        out_shape=[jax.ShapeDtypeStruct((LISTED, ROWS, BLK), jnp.float32)] * 2,
        in_specs=[pl.BlockSpec(memory_space=pltpu.SMEM)] + [vmem] * (1 + len(results)),
        out_specs=[anywhere] * 2,
        scratch_shapes=[
            pltpu.VMEM((2 * LISTED - LOCAL, ROWS, BLK), jnp.float32),
            pltpu.SemaphoreType.DMA((2 * LISTED,)),
        ],
        compiler_params=params(),
        cost_estimate=pl.CostEstimate(flops=1150000001, bytes_accessed=3000001, transcendentals=0),
        name="finish",
    )(table, cut, *results)


def after(values, others):
    count = len(values)
    return lax.optimization_barrier((*values, *others))[:count]


def body(densities, coulomb, pairs, owner):
    blocks = densities.reshape(STORED, BLK, densities.shape[1])
    weight = coulomb.reshape(1, -1)
    place = jnp.stack([lax.axis_index("trans"), lax.axis_index("pw")]).astype(jnp.int32)
    table = make_table(place, pairs.T, owner)

    def begin(lefts, start, count, table=table):
        own, up_add, down_add, up, down = products(table, blocks, weight, lefts, start, count)
        return own, up_add, down_add, along_y(up, 1), along_y(down, NY - 1)

    def carry_on(own, up_add, down_add, up, down):
        up_sum, down_sum = passed_on(up_add, down_add, up, down)
        return own, up, down, along_y(up_sum, 1), along_y(down_sum, NY - 1)

    near = select(NEAR_AT, 3, table, blocks)
    (ready,) = after((table,), near)
    near = [shifted(send, step) for step, send in zip((1, -1), near)]
    local = begin([], 0, LOCAL, ready)
    (ready,) = after((ready,), local[:1])
    far, last = select(FAR_AT, 2, ready, blocks), select(LAST_AT, 1, ready, blocks)
    own, up_add, down_add, up, down = local
    sums = passed_on(up_add, down_add, up, down)
    local = own, up, down, along_y(sums[0], 1), along_y(sums[1], NY - 1)
    near = after(near, (*last, *sums))
    far = [shifted(send, step) for step, send in zip((2, -2), after(far, near))]
    own, up_add, down_add, up, down = begin(near, NEAR_AT, 2 * MULT)
    sums = passed_on(up_add, down_add, up, down)
    parts_near = own, up, down, along_y(sums[0], 1), along_y(sums[1], NY - 1)
    last = [shifted(send, step) for step, send in zip((2, -2), after(last, far))]
    parts_far = carry_on(*begin(after(far, (*sums, *local[3:])), FAR_AT, LAST_AT - FAR_AT))
    parts_last = carry_on(*begin(after(last, parts_near[3:]), LAST_AT, LISTED - LAST_AT))
    keep, give = plane_sums(table, (after(local, parts_last[:1]), parts_near), MULT)
    stay, near_a, near_b, cut = totals(keep, across_z(give), 0, None)
    keep, give = plane_sums(table, (parts_far, parts_last), 2)
    far_a, far_b, cut = totals(keep, across_z(give), FAR_AT, cut)
    back = [shifted(array, -step) for array, step in zip((near_a, near_b, far_a, far_b), (1, -1, 2, -2))]
    kernel, kernel_t = finish(table, exchanged(cut), (stay, *back))
    return jnp.transpose(kernel, (1, 0, 2)), jnp.transpose(kernel_t, (1, 0, 2))


def solution(mesh):
    in_specs = (P("trans", "pw"), P("pw"), P(), P())
    out_specs = (P("pw", "trans", None), P("pw", "trans", None))
    return jax.shard_map(body, mesh=mesh, in_specs=in_specs, out_specs=out_specs, check_vma=False)
```
